512 devices in a mesh: section: 8 (over z_lo, core), slab: 64 (over x, z_hi, y).
Axes of the slice: x: 4, y: 8, z: 8 (z_hi: 2, z_lo: 4; z = z_hi * 4 + z_lo), core: 2. Of those that a mesh axis runs over, the one named last changes fastest.
Arguments:
- saved_in: bfloat16 [8, 128, 32, 8, 128], P('section', 'slab'), may hold values from -6 to 6
- saved_out: bfloat16 [8, 128, 32, 8, 128], P('section', 'slab'), as said below
- weights: bfloat16 [8, 27, 128, 128], P('section'), may hold values from -0.15625 to 0.15625
- cotangent: bfloat16 [128, 32, 8, 128], P('slab'), may hold values from -6 to 6
Outputs:
- act_grads: bfloat16 [8, 128, 32, 8, 128], P('section', 'slab')
- kernel_grads: float32 [8, 27, 128, 128], P('section')
- bias_grads: float32 [8, 128], P('section')
The draws below stay inside these ranges and needn't reach their ends.
Inputs may be any that keep to these rules, and one draw needn't show every extreme that they name: `saved_out`: every entry is zero or positive.
All inputs are finite; a program needn't handle non-finite values.
Results may differ from the reference program's by a relative error of at most 0.015.
Values may be sent and summed in bfloat16 or wider, within the bound.
A program may use at most 64 MiB of HBM per device.

```python
import jax
import jax.numpy as jnp

C = 128
XW = 32
ZD = 8
NY = 128
VOXELS = 32768
N_SECTION = 8


def draw_saved_out(key, part):
    key = jax.random.fold_in(key, 7)
    array_shape = (N_SECTION, NY, XW, ZD, C)
    values = jax.random.normal(key, array_shape, jnp.float32)
    return jnp.maximum(values, 0.0).astype(jnp.bfloat16)


def levels(own_key, extent, cuts, least, high):
    def one(axis_at, shards_of):
        heights = jax.random.uniform(jax.random.fold_in(jax.random.fold_in(own_key, 6), axis_at), (shards_of,), jnp.float32, least / len(cuts), high / len(cuts))
        return jnp.repeat(jnp.exp(heights), extent[axis_at] // shards_of).reshape((-1,) + (1,) * (len(extent) - axis_at - 1))

    loudness = one(*cuts[0])
    for cut in cuts[1:]:
        loudness = loudness * one(*cut)
    return loudness


def gaussian(stream_key, dims, scale, bound, shards=(), held_as=jnp.bfloat16):
    drawn = jax.random.normal(stream_key, dims, jnp.float32) * scale
    if len(shards) > 0:
        drawn = levels(stream_key, dims, shards, -0.22, 0.18) * drawn
    return jnp.clip(drawn, min=-bound, max=bound).astype(held_as)


def setup_inputs(seed: int = 0) -> dict:
    keys = jax.random.split(jax.random.key(seed), 5)
    saved_in = gaussian(keys[0], (N_SECTION, NY, XW, ZD, C), 1.0, 6.0, ((0, 8), (1, 64)))
    saved_out = draw_saved_out(jax.random.fold_in(keys[4], 71), 0)
    weights = gaussian(keys[2], (N_SECTION, 27, C, C), (27 * C // 2) ** -0.5, 0.15625, ((0, 8),))
    cotangent = gaussian(keys[3], (NY, XW, ZD, C), 1.0, 6.0, ((0, 64),))
    return {"saved_in": saved_in, "saved_out": saved_out, "weights": weights, "cotangent": cotangent}


def shifted(padded, start_y, start_x, start_z, rows_y, cells_x, cells_z):
    return padded[start_y:start_y + rows_y, start_x:start_x + cells_x, start_z:start_z + cells_z]


def reference(saved_in, saved_out, weights, cotangent):
    rows_y, cells_x, cells_z, channels = cotangent.shape
    norm_factor = 1.0 / (VOXELS ** 0.5)
    act_grads = [None] * N_SECTION
    kernel_grads = [None] * N_SECTION
    bias_grads = [None] * N_SECTION
    incoming = cotangent
    for level_index in reversed(range(N_SECTION)):
        masked = jnp.where(saved_out[level_index] > 0, incoming, jnp.zeros_like(incoming))
        padded_grad = jnp.pad(masked, ((1, 1), (1, 1), (1, 1), (0, 0)))
        padded_input = jnp.pad(saved_in[level_index], ((1, 1), (1, 1), (1, 1), (0, 0)))
        flat_grad = masked.reshape(-1, channels)
        summed = jnp.zeros((rows_y * cells_x * cells_z, channels), jnp.float32)
        blocks = []
        for offset in range(27):
            step_y = offset // 9 - 1
            step_x = offset // 3 % 3 - 1
            step_z = offset % 3 - 1
            source = shifted(padded_grad, 1 - step_y, 1 - step_x, 1 - step_z, rows_y, cells_x, cells_z).reshape(-1, channels)
            summed = summed + jnp.dot(source, weights[level_index, offset].T, preferred_element_type=jnp.float32)
            window = shifted(padded_input, 1 + step_y, 1 + step_x, 1 + step_z, rows_y, cells_x, cells_z).reshape(-1, channels)
            blocks.append(jnp.dot(window.T, flat_grad, preferred_element_type=jnp.float32))
        if level_index < N_SECTION // 2:
            summed = summed + act_grads[level_index + N_SECTION // 2].reshape(-1, channels).astype(jnp.float32)
        act_grads[level_index] = summed.reshape(rows_y, cells_x, cells_z, channels).astype(jnp.bfloat16)
        kernel_grads[level_index] = jnp.stack(blocks) * norm_factor
        bias_grads[level_index] = jnp.sum(masked.astype(jnp.float32), axis=(0, 1, 2)) * norm_factor
        incoming = act_grads[level_index]
    return jnp.stack(act_grads), jnp.stack(kernel_grads), jnp.stack(bias_grads)
```

```python
import math

import jax
import jax.numpy as jnp
from jax import lax
from jax.experimental import pallas as pl
from jax.experimental.pallas import tpu as pltpu
from jax.sharding import PartitionSpec as P

MESH = pl.DeviceIdType.MESH
F32 = jnp.float32
BF16 = jnp.bfloat16

RUN = 8
GROUPS = 8
CHUNK = 432
PART = 448


def kernel(
    si_ref, so_ref, w_ref, cot_ref,
    act_ref, kg_ref, bias_ref,
    inc, so6, act6, skip6, s0, s1, wst, sit, kgp, rsb, p2b, agb,
    halo_send, halo_recv, inc_send, inc_recv, skip_send, skip_recv,
    rs_send, rs_recv, p2_send, p2_recv, ag_send, ag_recv,
):
    sec = lax.axis_index("section")
    j = lax.axis_index("slab")
    n_sec = lax.axis_size("section")
    n_slab = lax.axis_size("slab")
    y = lax.rem(j, RUN)
    g = lax.div(j, RUN)
    odd = lax.rem(sec, 2) == 1
    even = lax.rem(sec, 2) == 0
    has_low = j > 0
    has_high = j < n_slab - 1
    top = sec == n_sec - 1

    def signal(s, t):
        pl.semaphore_signal(barrier, inc=1, device_id=(s, t), device_id_type=MESH)

    barrier = pltpu.get_barrier_semaphore()
    for d in range(1, RUN):
        signal(sec, g * RUN + lax.rem(y + d, RUN))
    for d in range(1, GROUPS):
        signal(sec, lax.rem(g + d, GROUPS) * RUN + y)

    @pl.when(jnp.logical_and(has_low, y == 0))
    def _():
        signal(sec, j - 1)

    @pl.when(jnp.logical_and(has_high, y == RUN - 1))
    def _():
        signal(sec, j + 1)

    @pl.when(sec > 0)
    def _():
        signal(sec - 1, j)

    @pl.when(jnp.logical_not(top))
    def _():
        signal(sec + 1, j)

    @pl.when(jnp.logical_and(even, jnp.logical_and(sec > 0, has_low)))
    def _():
        signal(sec - 1, j - 1)

    @pl.when(jnp.logical_and(even, jnp.logical_and(sec > 0, has_high)))
    def _():
        signal(sec - 1, j + 1)

    @pl.when(jnp.logical_and(odd, jnp.logical_and(jnp.logical_not(top), has_low)))
    def _():
        signal(sec + 1, j - 1)

    @pl.when(jnp.logical_and(odd, jnp.logical_and(jnp.logical_not(top), has_high)))
    def _():
        signal(sec + 1, j + 1)

    @pl.when(sec >= 4)
    def _():
        signal(sec - 4, j)

    @pl.when(sec < 4)
    def _():
        signal(sec + 4, j)

    def one(cond):
        return jnp.where(cond, 1, 0)

    diagonal = jnp.logical_or(
        jnp.logical_and(even, sec > 0), jnp.logical_and(odd, jnp.logical_not(top))
    )
    expected = (
        RUN - 1 + GROUPS - 1 + 1
        + one(jnp.logical_and(has_low, y == 0))
        + one(jnp.logical_and(has_high, y == RUN - 1))
        + one(sec > 0)
        + one(jnp.logical_not(top))
        + one(jnp.logical_and(diagonal, has_low))
        + one(jnp.logical_and(diagonal, has_high))
    )

    so = so_ref[...]
    so6[2:4] = so

    @pl.when(top)
    def _():
        so6[2:4] = jnp.where(so.astype(F32) > 0, cot_ref[...].astype(F32), 0.0).astype(BF16)

    @pl.when(jnp.logical_not(has_low))
    def _():
        so6[0:2] = jnp.zeros((2, 256, 128), BF16)

        @pl.when(odd)
        def _():
            inc[0:2] = jnp.zeros((2, 256, 128), BF16)

    @pl.when(jnp.logical_not(has_high))
    def _():
        so6[4:6] = jnp.zeros((2, 256, 128), BF16)

        @pl.when(odd)
        def _():
            inc[4:6] = jnp.zeros((2, 256, 128), BF16)

    pl.semaphore_wait(barrier, expected)

    def remote(src, dst, ss, rs, s, t):
        return pltpu.make_async_remote_copy(
            src_ref=src, dst_ref=dst, send_sem=ss, recv_sem=rs,
            device_id=(s, t), device_id_type=MESH,
        )

    def halo(low):
        own = so6.at[2:4]
        if low:
            return remote(own, so6.at[4:6], halo_send.at[0], halo_recv.at[0], sec, j - 1)
        return remote(own, so6.at[0:2], halo_send.at[1], halo_recv.at[1], sec, j + 1)

    @pl.when(has_low)
    def _():
        halo(True).start()

    @pl.when(has_high)
    def _():
        halo(False).start()

    def turn(c, carry):
        k = c
        tile = w_ref[k].astype(F32)
        wst[lax.div(k, 3), pl.ds(pl.multiple_of(lax.rem(k, 3) * 128, 128), 128), :] = tile.T.astype(BF16)
        return carry

    lax.fori_loop(0, 27, turn, 0)
    for r in range(4):
        sit[:, r * 128:(r + 1) * 128] = si_ref[
            r // 2, (r % 2) * 128:(r % 2) * 128 + 128
        ].astype(F32).T.astype(BF16)
    for r in range(6):
        s1[r, 0:16] = jnp.zeros((16, 384), BF16)
        s1[r, 256:272] = jnp.zeros((16, 384), BF16)

    @pl.when(has_low)
    def _():
        halo(False).wait_recv()

    @pl.when(has_high)
    def _():
        halo(True).wait_recv()

    def to_inc(which):
        own = act6.at[2:4]
        if which == 0:
            return remote(own, inc.at[2:4], inc_send.at[0], inc_recv.at[0], sec - 1, j)
        if which == 1:
            return remote(own, inc.at[4:6], inc_send.at[1], inc_recv.at[1], sec - 1, j - 1)
        if which == 2:
            return remote(own, inc.at[0:2], inc_send.at[2], inc_recv.at[2], sec - 1, j + 1)
        return remote(act6.at[1:5], inc.at[1:5], inc_send.at[0], inc_recv.at[3], sec - 1, j)

    def to_skip(rows):
        if rows == 4:
            return remote(act6.at[1:5], skip6.at[1:5], skip_send, skip_recv.at[0], sec - 4, j)
        return remote(act6.at[2:4], skip6.at[2:4], skip_send, skip_recv.at[1], sec - 4, j)

    @pl.when(jnp.logical_and(odd, jnp.logical_not(top)))
    def _():
        to_inc(0).wait_recv()

        @pl.when(has_high)
        def _():
            to_inc(1).wait_recv()

        @pl.when(has_low)
        def _():
            to_inc(2).wait_recv()

    @pl.when(even)
    def _():
        to_inc(3).wait_recv()

    depth = lax.rem(lax.broadcasted_iota(jnp.int32, (256, 128), 0), 8)

    def stack_row(r, carry):
        held = so6[r].astype(F32)
        arrived = jnp.where(held > 0, inc[r].astype(F32), 0.0)
        m = jnp.where(top, held, arrived)
        up = jnp.where(depth == 7, 0.0, pltpu.roll(m, 255, 0)).astype(BF16)
        down = jnp.where(depth == 0, 0.0, pltpu.roll(m, 1, 0)).astype(BF16)
        m = m.astype(BF16)
        s0[r, :, 0:128] = up
        s0[r, :, 128:256] = m
        s0[r, :, 256:384] = down
        s1[r, 8:264, 0:128] = up
        s1[r, 8:264, 128:256] = m
        s1[r, 8:264, 256:384] = down
        return carry

    @pl.when(odd)
    def _():
        lax.fori_loop(0, 6, stack_row, 0)

    @pl.when(even)
    def _():
        lax.fori_loop(1, 5, stack_row, 0)

    def shifted(r, dx):
        if dx == 0:
            return s0[r]
        if dx == 1:
            return s1[r, 0:256]
        return s1[r, 16:272]

    def conv_row(r, carry):
        acc = jnp.zeros((256, 128), F32)
        for dy in (-1, 0, 1):
            for dx in (-1, 0, 1):
                acc = acc + jnp.dot(
                    shifted(r - dy, dx), wst[3 * (dy + 1) + dx + 1], preferred_element_type=F32
                )
        out = jnp.where(sec < 4, acc + skip6[r].astype(F32), acc)
        act6[r] = out.astype(BF16)
        return carry

    def conv():
        @pl.when(jnp.logical_and(sec < 4, odd))
        def _():
            to_skip(4).wait_recv()

        @pl.when(jnp.logical_and(sec < 4, even))
        def _():
            to_skip(2).wait_recv()

        @pl.when(odd)
        def _():
            lax.fori_loop(1, 5, conv_row, 0)

        @pl.when(even)
        def _():
            lax.fori_loop(2, 4, conv_row, 0)

    @pl.when(sec > 0)
    def _():
        conv()

        @pl.when(odd)
        def _():
            to_inc(3).start()

        @pl.when(even)
        def _():
            to_inc(0).start()

            @pl.when(has_low)
            def _():
                to_inc(1).start()

            @pl.when(has_high)
            def _():
                to_inc(2).start()

        @pl.when(jnp.logical_and(sec >= 4, odd))
        def _():
            to_skip(4).start()

        @pl.when(jnp.logical_and(sec >= 4, even))
        def _():
            to_skip(2).start()

    for dy in (-1, 0, 1):
        for dx in (-1, 0, 1):
            rhs = jnp.concatenate([shifted(2 - dy, dx), shifted(3 - dy, dx)], axis=0)
            block = jnp.dot(sit[...], rhs, preferred_element_type=F32).astype(BF16)
            for dz in range(3):
                row = (9 * (dy + 1) + 3 * (dx + 1) + dz) * 128
                lo = row
                while lo < row + 128:
                    c = lo // CHUNK
                    hi = min(row + 128, (c + 1) * CHUNK)
                    kgp[c, lo - c * CHUNK:hi - c * CHUNK] = block[
                        lo - row:hi - row, dz * 128:(dz + 1) * 128
                    ]
                    lo = hi
    m = s0[2, :, 128:256].astype(F32) + s0[3, :, 128:256].astype(F32)

    def split(total):
        first = total.astype(BF16).astype(F32)
        rows = lax.broadcasted_iota(jnp.int32, (16, 128), 0)
        both = jnp.where(rows == 0, first, jnp.where(rows == 1, total - first, 0.0))
        return both.astype(BF16)

    bias_rows = split(jnp.sum(m, axis=0, keepdims=True))
    for c in range(RUN):
        kgp[c, CHUNK:PART] = bias_rows

    def rs(d):
        to = lax.rem(y + d, RUN)
        return remote(kgp.at[to], rsb.at[d], rs_send.at[d], rs_recv.at[d], sec, g * RUN + to)

    for d in range(1, RUN):
        rs(d).start()

    @pl.when(sec == 0)
    def _():
        conv()

    for d in range(1, RUN):
        rs(d).wait_recv()

    def piece(i, count):
        return pl.ds(pl.multiple_of(i * count, count), count)

    def add_run(i, carry):
        rows = piece(i, 48)
        total = kgp[y, rows].astype(F32)
        for d in range(1, RUN):
            total = total + rsb[d, rows].astype(F32)
        p2b[g, rows] = total.astype(BF16)
        return carry

    lax.fori_loop(0, CHUNK // 48, add_run, 0)
    total = kgp[y, CHUNK:PART].astype(F32)
    for d in range(1, RUN):
        total = total + rsb[d, CHUNK:PART].astype(F32)
    p2b[g, CHUNK:PART] = split(jnp.sum(total, axis=0, keepdims=True))

    def p2(d):
        to = lax.rem(g + d, GROUPS)
        return remote(p2b.at[g], p2b.at[g], p2_send.at[d], p2_recv.at[d], sec, to * RUN + y)

    def p2_in(d):
        source = lax.rem(g + GROUPS - d, GROUPS)
        return remote(p2b.at[source], p2b.at[source], p2_send.at[d], p2_recv.at[d], sec, source * RUN + y)

    for d in range(1, GROUPS):
        p2(d).start()
    for d in range(1, GROUPS):
        p2_in(d).wait_recv()

    def add_groups(i, carry):
        rows = piece(i, 48)
        total = p2b[0, rows].astype(F32)
        for d in range(1, GROUPS):
            total = total + p2b[d, rows].astype(F32)
        agb[y, rows] = total.astype(BF16)
        return carry

    lax.fori_loop(0, CHUNK // 48, add_groups, 0)

    def ag(d):
        to = lax.rem(y + d, RUN)
        return remote(agb.at[y], agb.at[y], ag_send.at[d], ag_recv.at[d], sec, g * RUN + to)

    def ag_in(d):
        source = lax.rem(y + RUN - d, RUN)
        return remote(agb.at[source], agb.at[source], ag_send.at[d], ag_recv.at[d], sec, g * RUN + source)

    for d in range(1, RUN):
        ag(d).start()

    total = p2b[0, CHUNK:PART].astype(F32)
    for d in range(1, GROUPS):
        total = total + p2b[d, CHUNK:PART].astype(F32)
    bias_ref[...] = jnp.broadcast_to(jnp.sum(total, axis=0, keepdims=True), (8, 128))
    act_ref[...] = act6[2:4]

    @pl.when(has_low)
    def _():
        halo(True).wait_send()

    @pl.when(has_high)
    def _():
        halo(False).wait_send()

    @pl.when(jnp.logical_and(sec > 0, odd))
    def _():
        to_inc(3).wait_send()

    @pl.when(jnp.logical_and(sec > 0, even))
    def _():
        to_inc(0).wait_send()

        @pl.when(has_low)
        def _():
            to_inc(1).wait_send()

        @pl.when(has_high)
        def _():
            to_inc(2).wait_send()

    @pl.when(jnp.logical_and(sec >= 4, odd))
    def _():
        to_skip(4).wait_send()

    @pl.when(jnp.logical_and(sec >= 4, even))
    def _():
        to_skip(2).wait_send()

    for d in range(1, RUN):
        rs(d).wait_send()
    for d in range(1, GROUPS):
        p2(d).wait_send()
    for d in range(1, RUN):
        ag(d).wait_send()
    for d in range(1, RUN):
        ag_in(d).wait_recv()
    kg_ref[...] = agb[...]


def local(saved_in, saved_out, weights, cotangent):
    rows_y, cells_x, cells_z, channels = cotangent.shape
    norm_factor = 1.0 / math.sqrt(rows_y * lax.axis_size("slab") * cells_x * cells_z)
    flat = (rows_y, cells_x * cells_z, channels)
    vmem = pl.BlockSpec(memory_space=pltpu.VMEM)
    six = pltpu.VMEM((6, 256, 128), BF16)
    sems = pltpu.SemaphoreType.DMA
    act, kg, bias = pl.pallas_call(
        kernel,
        name="backward",
        out_shape=(
            jax.ShapeDtypeStruct(flat, BF16),
            jax.ShapeDtypeStruct((RUN, CHUNK, channels), BF16),
            jax.ShapeDtypeStruct((8, channels), F32),
        ),
        in_specs=[vmem] * 4,
        out_specs=(vmem,) * 3,
        scratch_shapes=[
            six, six, six, six,
            pltpu.VMEM((6, 256, 384), BF16),
            pltpu.VMEM((6, 272, 384), BF16),
            pltpu.VMEM((9, 384, 128), BF16),
            pltpu.VMEM((128, 512), BF16),
            pltpu.VMEM((RUN, PART, 128), BF16),
            pltpu.VMEM((RUN, PART, 128), BF16),
            pltpu.VMEM((GROUPS, PART, 128), BF16),
            pltpu.VMEM((RUN, CHUNK, 128), BF16),
            sems((2,)), sems((2,)), sems((3,)), sems((4,)), sems, sems((2,)),
            sems((8,)), sems((8,)), sems((8,)), sems((8,)), sems((8,)), sems((8,)),
        ],
        compiler_params=pltpu.CompilerParams(
            collective_id=0, has_side_effects=True, vmem_limit_bytes=40 << 20
        ),
    )(
        saved_in[0].reshape(flat), saved_out[0].reshape(flat), weights[0], cotangent.reshape(flat)
    )
    kernel_sum = kg.reshape(27, channels, channels).astype(F32) * norm_factor
    bias_sum = bias[:1] * norm_factor
    return act.reshape((1,) + cotangent.shape), kernel_sum[None], bias_sum


def solution(mesh):
    placed = (
        P("section", "slab", None, None, None),
        P("section", "slab", None, None, None),
        P("section", None, None, None),
        P("slab", None, None, None),
    )
    return jax.shard_map(
        local,
        mesh=mesh,
        in_specs=placed,
        out_specs=(
            P("section", "slab", None, None, None),
            P("section", None, None, None),
            P("section", None),
        ),
        check_vma=False,
    )
```

```python
import math

import jax
import jax.numpy as jnp
from jax import lax
from jax.experimental import pallas as pl
from jax.experimental.pallas import tpu as pltpu
from jax.sharding import PartitionSpec as P

MESH = pl.DeviceIdType.MESH
F32 = jnp.float32
BF16 = jnp.bfloat16

RUN = 8
GROUPS = 8
SHARE = 16
PIECES = 7
AHEAD = 1


def kernel(
    si_ref, so_ref, w_ref, cot_ref,
    act_ref, kg_ref, bias_ref,
    wv, sov, cotv, inc, so6, act6, skip6, s9, w9, mt, mrun, lhs, srun, kgc, rsb, a1, a2,
    load, halo_send, halo_recv, inc_send, inc_recv, skip_send, skip_recv, go,
    si_send, si_recv, edge_send, edge_recv, relay_send, relay_recv,
    mx_send, mx_recv, rs_send, rs_recv,
    a1_send, a1_recv, b1_send, b1_recv, a2_send, a2_recv, b2_send, b2_recv,
):
    sec = lax.axis_index("section")
    j = lax.axis_index("slab")
    n_sec = lax.axis_size("section")
    n_slab = lax.axis_size("slab")
    y = lax.rem(j, RUN)
    g = lax.div(j, RUN)
    odd = lax.rem(sec, 2) == 1
    even = lax.rem(sec, 2) == 0
    has_low = j > 0
    has_high = j < n_slab - 1
    top = sec == n_sec - 1
    first = y == 0
    last = y == RUN - 1
    owner = g < PIECES

    def both(*conditions):
        out = conditions[0]
        for c in conditions[1:]:
            out = jnp.logical_and(out, c)
        return out

    def when(*conditions):
        return pl.when(both(*conditions))

    def loads():
        return (
            pltpu.make_async_copy(so_ref, sov, load.at[0]),
            pltpu.make_async_copy(cot_ref, cotv, load.at[1]),
            pltpu.make_async_copy(w_ref, wv, load.at[2]),
            pltpu.make_async_copy(si_ref, srun.at[pl.ds(1 + 2 * y, 2)], load.at[3]),
        )

    for c in loads():
        c.start()

    barrier = pltpu.get_barrier_semaphore()

    def signal(s, t):
        pl.semaphore_signal(barrier, inc=1, device_id=(s, t), device_id_type=MESH)

    @when(has_low, first)
    def _():
        signal(sec, j - 1)

    @when(has_high, last)
    def _():
        signal(sec, j + 1)

    for d in range(1, RUN):
        signal(sec, g * RUN + lax.rem(y + d, RUN))
    for d in range(1, GROUPS):
        signal(sec, lax.rem(g + d, GROUPS) * RUN + y)

    @when(sec > 0)
    def _():
        signal(sec - 1, j)

    @when(jnp.logical_not(top))
    def _():
        signal(sec + 1, j)

    @when(even, sec > 0, has_low)
    def _():
        signal(sec - 1, j - 1)

    @when(even, sec > 0, has_high)
    def _():
        signal(sec - 1, j + 1)

    @when(odd, jnp.logical_not(top), has_low)
    def _():
        signal(sec + 1, j - 1)

    @when(odd, jnp.logical_not(top), has_high)
    def _():
        signal(sec + 1, j + 1)

    @when(sec >= 4)
    def _():
        signal(sec - 4, j)

    @when(sec < 4)
    def _():
        signal(sec + 4, j)

    def one(*conditions):
        return jnp.where(both(*conditions), 1, 0)

    diagonal = jnp.logical_or(both(even, sec > 0), both(odd, jnp.logical_not(top)))
    expected = (
        RUN - 1 + GROUPS - 1 + 1
        + one(has_low, first) + one(has_high, last)
        + one(sec > 0) + one(jnp.logical_not(top))
        + one(diagonal, has_low) + one(diagonal, has_high)
    )

    blank = jnp.zeros((2, 256, 128), BF16)

    @when(jnp.logical_not(has_low))
    def _():
        so6[0:2] = blank

        @when(odd)
        def _():
            inc[0:2] = blank

    @when(jnp.logical_not(has_high))
    def _():
        so6[4:6] = blank

        @when(odd)
        def _():
            inc[4:6] = blank

    @when(g == 0)
    def _():
        srun[0] = blank[0]

    @when(g == GROUPS - 1)
    def _():
        srun[2 * RUN + 1] = blank[0]

    load_so, load_cot, load_w, load_si = loads()
    load_so.wait()
    load_cot.wait()

    @when(top)
    def _():
        so6[2:4] = jnp.where(sov[...].astype(F32) > 0, cotv[...].astype(F32), 0.0).astype(BF16)

    @when(jnp.logical_not(top))
    def _():
        so6[2:4] = sov[...]

    load_w.wait()

    def turn(k, carry):
        dy, dx, dz = lax.div(k, 9), lax.rem(lax.div(k, 3), 3), lax.rem(k, 3)
        tile = wv[k].astype(F32).T.astype(BF16)
        rows = pl.ds(pl.multiple_of(dx * 384 + dz * 128, 128), 128)
        w9[rows, pl.ds(pl.multiple_of(dy * 128, 128), 128)] = tile
        return carry

    lax.fori_loop(0, 27, turn, 0)
    load_si.wait()

    pl.semaphore_wait(barrier, expected)

    def remote(src, dst, ss, rs, s, t):
        return pltpu.make_async_remote_copy(
            src_ref=src, dst_ref=dst, send_sem=ss, recv_sem=rs,
            device_id=(s, t), device_id_type=MESH,
        )

    def halo(low):
        own = so6.at[2:4]
        if low:
            return remote(own, so6.at[4:6], halo_send.at[0], halo_recv.at[0], sec, j - 1)
        return remote(own, so6.at[0:2], halo_send.at[1], halo_recv.at[1], sec, j + 1)

    @when(has_low)
    def _():
        halo(True).start()

    @when(has_high)
    def _():
        halo(False).start()

    def mate(d):
        return lax.rem(y + d, RUN)

    def mate_in(d):
        return lax.rem(y + RUN - d, RUN)

    def peer(d):
        return lax.rem(g + d, GROUPS)

    def peer_in(d):
        return lax.rem(g + GROUPS - d, GROUPS)

    def si_out(d):
        own = srun.at[pl.ds(1 + 2 * y, 2)]
        return remote(own, own, si_send.at[d], si_recv.at[d], sec, g * RUN + mate(d))

    def si_in(d):
        rows = srun.at[pl.ds(1 + 2 * mate_in(d), 2)]
        return remote(rows, rows, si_send.at[d], si_recv.at[d], sec, g * RUN + mate_in(d))

    def edge(low):
        if low:
            return remote(srun.at[1], srun.at[2 * RUN + 1], edge_send.at[0], edge_recv.at[0], sec, j - 1)
        return remote(srun.at[2 * RUN], srun.at[0], edge_send.at[1], edge_recv.at[1], sec, j + 1)

    def relay(low, d):
        row = srun.at[0] if low else srun.at[2 * RUN + 1]
        i = 0 if low else 1
        return remote(row, row, relay_send.at[i, d], relay_recv.at[i], sec, g * RUN + mate(d))

    low_row = g > 0
    high_row = g < GROUPS - 1

    def gather_run():
        @when(first, low_row)
        def _():
            edge(True).start()

        @when(last, high_row)
        def _():
            edge(False).start()

        for d in range(1, RUN):
            si_out(d).start()

        @when(first, low_row)
        def _():
            edge(False).wait_recv()
            for d in range(1, RUN):
                relay(True, d).start()

        @when(last, high_row)
        def _():
            edge(True).wait_recv()
            for d in range(1, RUN):
                relay(False, d).start()

    @when(has_low)
    def _():
        halo(False).wait_recv()

    @when(has_high)
    def _():
        halo(True).wait_recv()

    early = sec < n_sec - 2
    late = sec >= n_sec - 2

    @when(early)
    def _():
        gather_run()

    def to_inc(which):
        own = act6.at[2:4]
        if which == 0:
            return remote(own, inc.at[2:4], inc_send.at[0], inc_recv.at[0], sec - 1, j)
        if which == 1:
            return remote(own, inc.at[4:6], inc_send.at[1], inc_recv.at[1], sec - 1, j - 1)
        if which == 2:
            return remote(own, inc.at[0:2], inc_send.at[2], inc_recv.at[2], sec - 1, j + 1)
        return remote(act6.at[1:5], inc.at[1:5], inc_send.at[0], inc_recv.at[3], sec - 1, j)

    def to_skip(rows):
        if rows == 4:
            return remote(act6.at[1:5], skip6.at[1:5], skip_send, skip_recv.at[0], sec - 4, j)
        return remote(act6.at[2:4], skip6.at[2:4], skip_send, skip_recv.at[1], sec - 4, j)

    @when(odd, jnp.logical_not(top))
    def _():
        to_inc(0).wait_recv()

        @when(has_high)
        def _():
            to_inc(1).wait_recv()

        @when(has_low)
        def _():
            to_inc(2).wait_recv()

    @when(even)
    def _():
        to_inc(3).wait_recv()

    depth = lax.broadcasted_iota(jnp.int32, (32, 8, 128), 1)
    edge_x = jnp.zeros((8, 128), F32)

    def stack_row(r, carry):
        held = so6[r].astype(F32)
        arrived = jnp.where(held > 0, inc[r].astype(F32), 0.0)
        m = jnp.where(top, held, arrived).reshape(32, 8, 128)
        up = jnp.where(depth == 7, 0.0, pltpu.roll(m, 7, 1)).reshape(256, 128)
        down = jnp.where(depth == 0, 0.0, pltpu.roll(m, 1, 1)).reshape(256, 128)
        for b, v in enumerate((up, m.reshape(256, 128), down)):
            at = b * 128
            s9[r, :, at:at + 128] = jnp.concatenate([v[8:], edge_x], 0).astype(BF16)
            s9[r, :, at + 384:at + 512] = v.astype(BF16)
            s9[r, :, at + 768:at + 896] = jnp.concatenate([edge_x, v[:-8]], 0).astype(BF16)
        return carry

    @when(odd)
    def _():
        lax.fori_loop(0, 6, stack_row, 0)

    @when(even)
    def _():
        lax.fori_loop(1, 5, stack_row, 0)

    def conv_rows(lo, hi):
        sums = {}
        for t in range(lo - 1, hi + 1):
            reach = [dy for dy in (-1, 0, 1) if lo <= t + dy < hi]
            p = jnp.dot(
                s9[t], w9[:, (reach[0] + 1) * 128:(reach[-1] + 2) * 128],
                preferred_element_type=F32,
            )
            for i, dy in enumerate(reach):
                v = p[:, i * 128:(i + 1) * 128]
                sums[t + dy] = v if dy == 1 or t + dy not in sums else sums[t + dy] + v
            r = t - 1
            if lo <= r < hi:
                act6[r] = jnp.where(sec < 4, sums[r] + skip6[r].astype(F32), sums[r]).astype(BF16)

    def conv():
        @when(sec < 4, odd)
        def _():
            to_skip(4).wait_recv()

        @when(sec < 4, even)
        def _():
            to_skip(2).wait_recv()

        @when(odd)
        def _():
            conv_rows(1, 5)

        @when(even)
        def _():
            conv_rows(2, 4)

    @when(sec > 0)
    def _():
        conv()

        @when(odd)
        def _():
            to_inc(3).start()

        @when(even)
        def _():
            to_inc(0).start()

            @when(has_low)
            def _():
                to_inc(1).start()

            @when(has_high)
            def _():
                to_inc(2).start()

    for r in range(2):
        for h in range(2):
            block = s9[2 + r, h * 128:(h + 1) * 128, 512:640].astype(F32).T.astype(BF16)
            at = r * 256 + h * 128
            mt[:, :, at:at + 128] = block.reshape(RUN, SHARE, 128)

    @when(even, sec > 0)
    def _():
        to_inc(0).wait_send()

        @when(has_low)
        def _():
            to_inc(1).wait_send()

        @when(has_high)
        def _():
            to_inc(2).wait_send()

        pl.semaphore_signal(go, inc=1, device_id=(sec + 1, j), device_id_type=MESH)

    @when(odd, sec > 1)
    def _():
        pl.semaphore_wait(go, 1)

    @when(sec >= 4, odd)
    def _():
        to_skip(4).start()

    @when(sec >= 4, even)
    def _():
        to_skip(2).start()

    def mx_out(d):
        return remote(mt.at[mate(d)], mrun.at[y], mx_send.at[d], mx_recv.at[d], sec, g * RUN + mate(d))

    def mx_in(d):
        return remote(mt.at[y], mrun.at[mate_in(d)], mx_send.at[d], mx_recv.at[d], sec, g * RUN + mate_in(d))

    for d in range(1, RUN):
        mx_out(d).start()
    mrun[y] = mt[y]

    @when(sec == 0)
    def _():
        conv()

    @when(late)
    def _():
        gather_run()

    lane = lax.broadcasted_iota(jnp.int32, (SHARE, 512), 1)
    cell_x = lax.rem(lax.div(lane, 8), 32)
    cell_z = lax.rem(lane, 8)
    fits = []
    for dx in (-1, 0, 1):
        for dz in (-1, 0, 1):
            fits.append(both(cell_x - dx >= 0, cell_x - dx < 32, cell_z - dz >= 0, cell_z - dz < 8))

    for d in range(1, RUN):
        mx_in(d).wait_recv()

    bias = jnp.zeros((SHARE, 512), F32)
    for u in range(RUN):
        m = mrun[u].astype(F32)
        bias = bias + m
        for i, ok in enumerate(fits):
            step = ((i // 3 - 1) * 8 + i % 3 - 1) % 512
            moved = m if step == 0 else jnp.where(ok, pltpu.roll(m, step, 1), 0.0)
            lhs[i * SHARE:(i + 1) * SHARE, u * 512:(u + 1) * 512] = moved.astype(BF16)

    for d in range(1, RUN):
        si_in(d).wait_recv()

    @when(low_row, jnp.logical_not(first))
    def _():
        relay(True, 1).wait_recv()

    @when(high_row, jnp.logical_not(last))
    def _():
        relay(False, 1).wait_recv()

    column = lax.broadcasted_iota(jnp.int32, (SHARE, 128), 1)

    def split(total):
        head = total.astype(BF16).astype(F32)
        return jnp.where(column == 0, head, jnp.where(column == 1, total - head, 0.0))

    for dy in range(3):
        block = jnp.dot(
            lhs[...], srun[dy:dy + 2 * RUN].reshape(RUN * 512, 128), preferred_element_type=F32
        ).astype(BF16)
        for i in range(9):
            t = dy * 9 + i
            kgc[t // 4, t % 4] = block[i * SHARE:(i + 1) * SHARE]
    kgc[6, 3] = split(jnp.sum(bias, axis=1, keepdims=True)).astype(BF16)

    def rs_out(d):
        return remote(
            kgc.at[peer(d)], rsb.at[d], rs_send.at[d], rs_recv.at[d], sec, peer(d) * RUN + y
        )

    def rs_in(d):
        return remote(
            kgc.at[0], rsb.at[d], rs_send.at[d], rs_recv.at[d], sec, peer_in(d) * RUN + y
        )

    for d in range(1, GROUPS):
        @when(peer(d) < PIECES)
        def _():
            rs_out(d).start()

    def a1_out(d):
        part = a1.at[y, g]
        return remote(part, part, a1_send.at[d], a1_recv.at[d], sec, peer(d) * RUN + y)

    def a1_in(d):
        part = a1.at[y, peer_in(d)]
        return remote(part, part, a1_send.at[d], a1_recv.at[d], sec, peer_in(d) * RUN + y)

    def b1_out(d):
        return remote(a1.at[y], a1.at[y], b1_send.at[d], b1_recv.at[d], sec, g * RUN + mate(d))

    def b1_in(d):
        part = a1.at[mate_in(d)]
        return remote(part, part, b1_send.at[d], b1_recv.at[d], sec, g * RUN + mate_in(d))

    def a2_out(d):
        part = a2.at[g, y]
        return remote(part, part, a2_send.at[d], a2_recv.at[d], sec, g * RUN + mate(d))

    def a2_in(d):
        part = a2.at[g, mate_in(d)]
        return remote(part, part, a2_send.at[d], a2_recv.at[d], sec, g * RUN + mate_in(d))

    def b2_out(d):
        return remote(a2.at[g], a2.at[g], b2_send.at[d], b2_recv.at[d], sec, peer(d) * RUN + y)

    def b2_in(d):
        part = a2.at[peer_in(d)]
        return remote(part, part, b2_send.at[d], b2_recv.at[d], sec, peer_in(d) * RUN + y)

    @when(owner)
    def _():
        for d in range(1, GROUPS):
            rs_in(d).wait_recv()
        total = kgc[g].astype(F32)
        for d in range(1, GROUPS):
            total = total + rsb[d].astype(F32)
        pair = split(total[3, :, 0:1] + total[3, :, 1:2])
        final = jnp.where(g == PIECES - 1, pair, total[3])
        a1[y, g] = total[:AHEAD].astype(BF16)
        a2[g, y, 0:3 - AHEAD] = total[AHEAD:3].astype(BF16)
        a2[g, y, 3 - AHEAD] = final.astype(BF16)
        for d in range(1, GROUPS):
            a1_out(d).start()
        for d in range(1, RUN):
            a2_out(d).start()

    act_ref[...] = act6[2:4]

    @when(owner)
    def _():
        for d in range(1, RUN):
            a2_in(d).wait_recv()
        for d in range(1, GROUPS):
            b2_out(d).start()

    for d in range(1, GROUPS):
        @when(peer_in(d) < PIECES)
        def _():
            a1_in(d).wait_recv()
    for d in range(1, RUN):
        b1_out(d).start()

    @when(has_low)
    def _():
        halo(True).wait_send()

    @when(has_high)
    def _():
        halo(False).wait_send()

    @when(first, low_row)
    def _():
        edge(True).wait_send()
        for d in range(1, RUN):
            relay(True, d).wait_send()

    @when(last, high_row)
    def _():
        edge(False).wait_send()
        for d in range(1, RUN):
            relay(False, d).wait_send()

    @when(sec > 0, odd)
    def _():
        to_inc(3).wait_send()

    @when(sec >= 4, odd)
    def _():
        to_skip(4).wait_send()

    @when(sec >= 4, even)
    def _():
        to_skip(2).wait_send()

    for d in range(1, RUN):
        si_out(d).wait_send()
        mx_out(d).wait_send()

        @when(peer(d) < PIECES)
        def _():
            rs_out(d).wait_send()

    @when(owner)
    def _():
        for d in range(1, RUN):
            a1_out(d).wait_send()
            a2_out(d).wait_send()
            b2_out(d).wait_send()

    for d in range(1, RUN):
        b1_out(d).wait_send()
    for d in range(1, RUN):
        b1_in(d).wait_recv()
    for d in range(1, GROUPS):
        @when(peer_in(d) < PIECES)
        def _():
            b2_in(d).wait_recv()

    for t in range(28):
        q, i = t // 4, t % 4
        if i < AHEAD:
            tile = a1[:, q, i]
        else:
            tile = a2[q, :, i - AHEAD]
        tile = tile.reshape(128, 128).astype(F32).T
        if t < 27:
            kg_ref[t] = tile.astype(BF16)
        else:
            bias_ref[...] = jnp.broadcast_to(tile[0:1] + tile[1:2], (8, 128))


def local(saved_in, saved_out, weights, cotangent):
    rows_y, cells_x, cells_z, channels = cotangent.shape
    norm_factor = 1.0 / math.sqrt(rows_y * lax.axis_size("slab") * cells_x * cells_z)
    flat = (rows_y, cells_x * cells_z, channels)
    vmem = pl.BlockSpec(memory_space=pltpu.VMEM)
    hbm = pl.BlockSpec(memory_space=pl.ANY)
    six = pltpu.VMEM((6, 256, 128), BF16)
    two = pltpu.VMEM((2, 256, 128), BF16)
    sems = pltpu.SemaphoreType.DMA
    act, kg, bias = pl.pallas_call(
        kernel,
        name="backward",
        out_shape=(
            jax.ShapeDtypeStruct(flat, BF16),
            jax.ShapeDtypeStruct((27, channels, channels), BF16),
            jax.ShapeDtypeStruct((8, channels), F32),
        ),
        in_specs=[hbm] * 4,
        out_specs=(vmem,) * 3,
        scratch_shapes=[
            pltpu.VMEM((27, 128, 128), BF16), two, two,
            six, six, six, six,
            pltpu.VMEM((6, 256, 1152), BF16),
            pltpu.VMEM((1152, 384), BF16),
            pltpu.VMEM((RUN, SHARE, 512), BF16),
            pltpu.VMEM((RUN, SHARE, 512), BF16),
            pltpu.VMEM((9 * SHARE, RUN * 512), BF16),
            pltpu.VMEM((2 * RUN + 2, 256, 128), BF16),
            pltpu.VMEM((PIECES, 4, SHARE, 128), BF16),
            pltpu.VMEM((GROUPS, 4, SHARE, 128), BF16),
            pltpu.VMEM((RUN, PIECES, AHEAD, SHARE, 128), BF16),
            pltpu.VMEM((PIECES, RUN, 4 - AHEAD, SHARE, 128), BF16),
            sems((4,)), sems((2,)), sems((2,)), sems((3,)), sems((4,)), sems, sems((2,)),
            pltpu.SemaphoreType.REGULAR,
            sems((8,)), sems((8,)), sems((2,)), sems((2,)), sems((2, 8)), sems((2,)),
            sems((8,)), sems((8,)), sems((8,)), sems((8,)),
            sems((8,)), sems((8,)), sems((8,)), sems((8,)),
            sems((8,)), sems((8,)), sems((8,)), sems((8,)),
        ],
        compiler_params=pltpu.CompilerParams(
            collective_id=0, has_side_effects=True, vmem_limit_bytes=56 << 20
        ),
    )(
        saved_in[0].reshape(flat), saved_out[0].reshape(flat), weights[0], cotangent.reshape(flat)
    )
    kernel_sum = kg.astype(F32) * norm_factor
    bias_sum = bias[:1] * norm_factor
    return act.reshape((1,) + cotangent.shape), kernel_sum[None], bias_sum


def solution(mesh):
    placed = (
        P("section", "slab", None, None, None),
        P("section", "slab", None, None, None),
        P("section", None, None, None),
        P("slab", None, None, None),
    )
    return jax.shard_map(
        local,
        mesh=mesh,
        in_specs=placed,
        out_specs=(
            P("section", "slab", None, None, None),
            P("section", None, None, None),
            P("section", None),
        ),
        check_vma=False,
    )
```

```python
import functools
import math

import jax
import jax.numpy as jnp
from jax import lax
from jax.experimental import pallas as pl
from jax.experimental.pallas import tpu as pltpu
from jax.sharding import PartitionSpec as P

MESH = pl.DeviceIdType.MESH
F32 = jnp.float32
BF16 = jnp.bfloat16

RUN = 8
GROUPS = 8
SHARE = 16
WIDE = 4
TILES = 7
AHEAD = 2


def kernel(
    si_ref, so_ref, w_ref, cot_ref,
    act_ref, a1, a2,
    wv, sov, cotv, inc, so6, act6, skip6, s9, w9, mt, mtx, mrun, ends, lhs, srun, kgc, rsb,
    load, halo_send, halo_recv, row_send, row_recv, slab_send, slab_recv, skip_send, skip_recv, go,
    up_send, up_recv, down_send, down_recv, end_send, end_recv,
    mx_send, mx_recv, rs_send, rs_recv,
    a1_send, a1_recv, b1_send, b1_recv, a2_send, a2_recv, b2_send, b2_recv,
):
    sec = lax.axis_index("section")
    j = lax.axis_index("slab")
    n_sec = lax.axis_size("section")
    n_slab = lax.axis_size("slab")
    y = lax.rem(j, RUN)
    g = lax.div(j, RUN)
    odd = lax.rem(sec, 2) == 1
    even = lax.rem(sec, 2) == 0
    has_low = j > 0
    has_high = j < n_slab - 1
    top = sec == n_sec - 1
    first = y == 0
    last = y == RUN - 1
    x = lax.div(g, 2)
    high = lax.rem(g, 2)

    def both(*conditions):
        out = conditions[0]
        for c in conditions[1:]:
            out = jnp.logical_and(out, c)
        return out

    def when(*conditions):
        return pl.when(both(*conditions))

    def loads():
        return (
            pltpu.make_async_copy(so_ref, sov, load.at[0]),
            pltpu.make_async_copy(cot_ref, cotv, load.at[1]),
            pltpu.make_async_copy(w_ref, wv, load.at[2]),
            pltpu.make_async_copy(si_ref, srun.at[pl.ds(2 * y, 2)], load.at[3]),
        )

    for c in loads():
        c.start()

    barrier = pltpu.get_barrier_semaphore()

    def signal(s, t):
        pl.semaphore_signal(barrier, inc=1, device_id=(s, t), device_id_type=MESH)

    @when(has_low, first)
    def _():
        signal(sec, j - 1)

    @when(has_high, last)
    def _():
        signal(sec, j + 1)

    for d in range(1, RUN):
        signal(sec, g * RUN + lax.rem(y + d, RUN))
    for d in range(1, GROUPS):
        signal(sec, lax.rem(g + d, GROUPS) * RUN + y)

    @when(sec > 0)
    def _():
        signal(sec - 1, j)

    @when(jnp.logical_not(top))
    def _():
        signal(sec + 1, j)

    @when(even, sec > 0, has_low)
    def _():
        signal(sec - 1, j - 1)

    @when(even, sec > 0, has_high)
    def _():
        signal(sec - 1, j + 1)

    @when(odd, jnp.logical_not(top), has_low)
    def _():
        signal(sec + 1, j - 1)

    @when(odd, jnp.logical_not(top), has_high)
    def _():
        signal(sec + 1, j + 1)

    @when(sec >= 4)
    def _():
        signal(sec - 4, j)

    @when(sec < 4)
    def _():
        signal(sec + 4, j)

    def one(*conditions):
        return jnp.where(both(*conditions), 1, 0)

    diagonal = jnp.logical_or(both(even, sec > 0), both(odd, jnp.logical_not(top)))
    expected = (
        RUN - 1 + GROUPS - 1 + 1
        + one(has_low, first) + one(has_high, last)
        + one(sec > 0) + one(jnp.logical_not(top))
        + one(diagonal, has_low) + one(diagonal, has_high)
    )

    blank = jnp.zeros((2, 256, 128), BF16)

    @when(jnp.logical_not(has_low))
    def _():
        so6[0:2] = blank

        @when(odd)
        def _():
            inc[0:2] = blank

    @when(jnp.logical_not(has_high))
    def _():
        so6[4:6] = blank

        @when(odd)
        def _():
            inc[4:6] = blank

    @when(g == 0)
    def _():
        ends[0] = jnp.zeros((SHARE, 256), BF16)

    @when(g == GROUPS - 1)
    def _():
        ends[1] = jnp.zeros((SHARE, 256), BF16)

    load_so, load_cot, load_w, load_si = loads()
    load_so.wait()
    load_cot.wait()

    @when(top)
    def _():
        so6[2:4] = jnp.where(sov[...].astype(F32) > 0, cotv[...].astype(F32), 0.0).astype(BF16)

    @when(jnp.logical_not(top))
    def _():
        so6[2:4] = sov[...]

    load_w.wait()

    def turn(k, carry):
        dy, dx, dz = lax.div(k, 9), lax.rem(lax.div(k, 3), 3), lax.rem(k, 3)
        tile = wv[k].astype(F32).T.astype(BF16)
        rows = pl.ds(pl.multiple_of(dx * 384 + dz * 128, 128), 128)
        w9[rows, pl.ds(pl.multiple_of(dy * 128, 128), 128)] = tile
        return carry

    lax.fori_loop(0, 27, turn, 0)
    load_si.wait()

    pl.semaphore_wait(barrier, expected)

    def remote(src, dst, ss, rs, s, t):
        return pltpu.make_async_remote_copy(
            src_ref=src, dst_ref=dst, send_sem=ss, recv_sem=rs,
            device_id=(s, t), device_id_type=MESH,
        )

    def halo(low):
        own = so6.at[2:4]
        if low:
            return remote(own, so6.at[4:6], halo_send.at[0], halo_recv.at[0], sec, j - 1)
        return remote(own, so6.at[0:2], halo_send.at[1], halo_recv.at[1], sec, j + 1)

    @when(has_low)
    def _():
        halo(True).start()

    @when(has_high)
    def _():
        halo(False).start()

    def mate(d):
        return lax.rem(y + d, RUN)

    def mate_in(d):
        return lax.rem(y + RUN - d, RUN)

    def peer(d):
        return lax.rem(g + d, GROUPS)

    def peer_in(d):
        return lax.rem(g + GROUPS - d, GROUPS)

    def rows_of(origin):
        return srun.at[pl.ds(2 * origin, 2)]

    def up_out(step):
        rows = rows_of(lax.rem(y + RUN - step, RUN))
        return remote(rows, rows, up_send.at[step], up_recv.at[step], sec, g * RUN + mate(1))

    def up_in(step):
        rows = rows_of(lax.rem(y + RUN - step - 1, RUN))
        return remote(rows, rows, up_send.at[step], up_recv.at[step], sec, g * RUN + mate(1))

    def down_out(step):
        rows = rows_of(lax.rem(y + step, RUN))
        return remote(rows, rows, down_send.at[step], down_recv.at[step], sec, g * RUN + mate(RUN - 1))

    def down_in(step):
        rows = rows_of(lax.rem(y + step + 1, RUN))
        return remote(rows, rows, down_send.at[step], down_recv.at[step], sec, g * RUN + mate(RUN - 1))

    low_row = g > 0
    high_row = g < GROUPS - 1

    def gather_run():
        for step in range(4):
            up_out(step).start()
            if step < 3:
                down_out(step).start()
            up_in(step).wait_recv()
            if step < 3:
                down_in(step).wait_recv()

    def halo_wait(low):
        if low:
            @when(has_low)
            def _():
                halo(False).wait_recv()
        else:
            @when(has_high)
            def _():
                halo(True).wait_recv()

    early = sec < n_sec - 2
    late = sec >= n_sec - 2

    @when(early)
    def _():
        gather_run()

    def to_sibling(r):
        return remote(act6.at[r], inc.at[r], row_send.at[r - 1], row_recv.at[r - 1], sec - 1, j)

    def to_slab(i, which):
        at = (2, 4, 0)[which] + i
        k = 3 * i + which
        return remote(
            act6.at[2 + i], inc.at[at], slab_send.at[k], slab_recv.at[k], sec - 1, j + (0, -1, 1)[which]
        )

    def slab_sends(i, act):
        getattr(to_slab(i, 0), act)()

        @when(has_low)
        def _():
            getattr(to_slab(i, 1), act)()

        @when(has_high)
        def _():
            getattr(to_slab(i, 2), act)()

    def to_skip(rows):
        if rows == 4:
            return remote(act6.at[1:5], skip6.at[1:5], skip_send, skip_recv.at[0], sec - 4, j)
        return remote(act6.at[2:4], skip6.at[2:4], skip_send, skip_recv.at[1], sec - 4, j)

    depth = lax.broadcasted_iota(jnp.int32, (32, 8, 128), 1)
    edge_x = jnp.zeros((8, 128), F32)

    def stack_row(r, carry):
        held = so6[r].astype(F32)
        arrived = jnp.where(held > 0, inc[r].astype(F32), 0.0)
        m = jnp.where(top, held, arrived).reshape(32, 8, 128)
        up = jnp.where(depth == 7, 0.0, pltpu.roll(m, 7, 1)).reshape(256, 128)
        down = jnp.where(depth == 0, 0.0, pltpu.roll(m, 1, 1)).reshape(256, 128)
        for b, v in enumerate((up, m.reshape(256, 128), down)):
            at = b * 128
            s9[r, :, at:at + 128] = jnp.concatenate([v[8:], edge_x], 0).astype(BF16)
            s9[r, :, at + 384:at + 512] = v.astype(BF16)
            s9[r, :, at + 768:at + 896] = jnp.concatenate([edge_x, v[:-8]], 0).astype(BF16)
        return carry

    def layer(lo, hi, steps, done):
        sums, count = {}, {}
        for ready, rows in steps:
            ready()
            for t in rows:
                reach = [dy for dy in (-1, 0, 1) if lo <= t + dy < hi]
                p = jnp.dot(
                    s9[t], w9[:, (reach[0] + 1) * 128:(reach[-1] + 2) * 128],
                    preferred_element_type=F32,
                )
                for i, dy in enumerate(reach):
                    r = t + dy
                    v = p[:, i * 128:(i + 1) * 128]
                    sums[r] = sums[r] + v if r in sums else v
                    count[r] = count.get(r, 0) + 1
                    if count[r] == 3:
                        total = sums.pop(r)
                        total = jnp.where(sec < 4, total + skip6[r].astype(F32), total)
                        act6[r] = total.astype(BF16)
                        done(r)

    def odd_layer(low_first):
        def own():
            @when(jnp.logical_not(top))
            def _():
                to_slab(0, 0).wait_recv()
                to_slab(1, 0).wait_recv()

            lax.fori_loop(2, 4, stack_row, 0)

        def side(low):
            halo_wait(low)

            @when(jnp.logical_not(top), has_low if low else has_high)
            def _():
                for i in range(2):
                    to_slab(i, 2 if low else 1).wait_recv()

            at = 0 if low else 4
            lax.fori_loop(at, at + 2, stack_row, 0)

        @when(sec < 4)
        def _():
            to_skip(4).wait_recv()

        lows = (lambda: side(True), (0, 1))
        highs = (lambda: side(False), (4, 5))
        order = [lows, highs] if low_first else [highs, lows]
        layer(1, 5, [(own, (2, 3))] + order, lambda r: to_sibling(r).start())

    def even_layer(low_first):
        rows = (1, 2, 3, 4) if low_first else (4, 3, 2, 1)

        def ready(r):
            to_sibling(r).wait_recv()
            lax.fori_loop(r, r + 1, stack_row, 0)

        @when(sec < 4)
        def _():
            to_skip(2).wait_recv()

        layer(
            2, 4, [(lambda r=r: ready(r), (r,)) for r in rows],
            lambda r: slab_sends(r - 2, "start"),
        )

    @when(odd, first)
    def _():
        odd_layer(False)

    @when(odd, jnp.logical_not(first))
    def _():
        odd_layer(True)

    @when(even)
    def _():
        halo_wait(True)
        halo_wait(False)

    @when(even, sec > 0, first)
    def _():
        even_layer(False)

    @when(even, sec > 0, jnp.logical_not(first))
    def _():
        even_layer(True)

    @when(sec == 0)
    def _():
        for r in range(1, 5):
            to_sibling(r).wait_recv()
        lax.fori_loop(1, 5, stack_row, 0)

    def turned(r, h):
        block = s9[r, h * 128:(h + 1) * 128, 512:640].astype(F32).T.astype(BF16)
        return block.reshape(RUN, SHARE, 128)

    for r in range(2):
        for h in range(2):
            at = r * 256 + h * 128
            mt[:, :, at:at + 128] = turned(2 + r, h)

    for outer, r in ((both(first, low_row), 1), (both(last, high_row), 4)):
        @when(outer)
        def _():
            for h in range(2):
                mtx[:, :, h * 128:(h + 1) * 128] = turned(r, h)

    @when(even, sec > 0)
    def _():
        slab_sends(0, "wait_send")
        slab_sends(1, "wait_send")
        pl.semaphore_signal(go, inc=1, device_id=(sec + 1, j), device_id_type=MESH)

    @when(odd, sec > 1)
    def _():
        pl.semaphore_wait(go, 1)

    @when(sec >= 4, odd)
    def _():
        to_skip(4).start()

    @when(sec >= 4, even)
    def _():
        to_skip(2).start()

    def mx_out(d):
        return remote(mt.at[mate(d)], mrun.at[y], mx_send.at[d], mx_recv.at[d], sec, g * RUN + mate(d))

    def mx_in(d):
        return remote(mt.at[y], mrun.at[mate_in(d)], mx_send.at[d], mx_recv.at[d], sec, g * RUN + mate_in(d))

    def end_out(i, d):
        return remote(mtx.at[mate(d)], ends.at[i], end_send.at[d], end_recv.at[i], sec, g * RUN + mate(d))

    for d in range(1, RUN):
        mx_out(d).start()
    mrun[y] = mt[y]

    has_end = (both(first, low_row), both(last, high_row))
    for i in range(2):
        @when(has_end[i])
        def _():
            for d in range(1, RUN):
                end_out(i, d).start()
            ends[i] = mtx[y]

    @when(sec == 0)
    def _():
        to_skip(2).wait_recv()
        layer(2, 4, [(lambda: None, (1, 2, 3, 4))], lambda r: None)

    @when(late)
    def _():
        gather_run()

    lane = lax.broadcasted_iota(jnp.int32, (SHARE, 512), 1)
    cell_x = lax.rem(lax.div(lane, 8), 32)
    cell_z = lax.rem(lane, 8)
    fits = []
    for dx in (-1, 0, 1):
        for dz in (-1, 0, 1):
            fits.append(both(cell_x - dx >= 0, cell_x - dx < 32, cell_z - dz >= 0, cell_z - dz < 8))

    for d in range(1, RUN):
        mx_in(d).wait_recv()

    for i, (there, away) in enumerate(((low_row, y > 0), (high_row, y < RUN - 1))):
        @when(there, away)
        def _():
            end_out(i, 1).wait_recv()

    def spread(m, at, width):
        for i, ok in enumerate(fits):
            step = ((i // 3 - 1) * 8 + i % 3 - 1) % width
            moved = m if step == 0 else jnp.where(ok[:, :width], pltpu.roll(m, step, 1), 0.0)
            lhs[i * SHARE:(i + 1) * SHARE, at:at + width] = moved.astype(BF16)

    bias = jnp.zeros((SHARE, 512), F32)
    spread(ends[0].astype(F32), 0, 256)
    for u in range(RUN):
        m = mrun[u].astype(F32)
        bias = bias + m
        spread(m, 256 + u * 512, 512)
    spread(ends[1].astype(F32), 256 + RUN * 512, 256)

    column = lax.broadcasted_iota(jnp.int32, (SHARE, 128), 1)

    def split(total):
        head = total.astype(BF16).astype(F32)
        return jnp.where(column == 0, head, jnp.where(column == 1, total - head, 0.0))

    for dy in range(3):
        block = jnp.dot(
            lhs[:, (2 - dy) * 256:(2 - dy) * 256 + RUN * 512],
            srun[...].reshape(RUN * 512, 128), preferred_element_type=F32,
        ).astype(BF16)
        for i in range(9):
            t = dy * 9 + i
            kgc[t // TILES, t % TILES] = block[i * SHARE:(i + 1) * SHARE]
    kgc[WIDE - 1, TILES - 1] = split(jnp.sum(bias, axis=1, keepdims=True)).astype(BF16)

    def rs_out(d):
        return remote(
            kgc.at[lax.div(peer(d), 2)], rsb.at[g], rs_send.at[d], rs_recv.at[d], sec, peer(d) * RUN + y
        )

    def rs_in(d):
        return remote(
            kgc.at[0], rsb.at[peer_in(d)], rs_send.at[d], rs_recv.at[d], sec, peer_in(d) * RUN + y
        )

    for d in range(1, GROUPS):
        rs_out(d).start()
    rsb[g] = kgc[x]

    def beside(d):
        return lax.rem(x + d, WIDE)

    def beside_in(d):
        return lax.rem(x + WIDE - d, WIDE)

    def across(at):
        return (2 * at + high) * RUN + y

    def a1_out(d):
        part = a1.at[y, x]
        return remote(part, part, a1_send.at[d], a1_recv.at[d], sec, across(beside(d)))

    def a1_in(d):
        part = a1.at[y, beside_in(d)]
        return remote(part, part, a1_send.at[d], a1_recv.at[d], sec, across(beside_in(d)))

    def b1_out(d):
        return remote(a1.at[y], a1.at[y], b1_send.at[d], b1_recv.at[d], sec, g * RUN + mate(d))

    def b1_in(d):
        part = a1.at[mate_in(d)]
        return remote(part, part, b1_send.at[d], b1_recv.at[d], sec, g * RUN + mate_in(d))

    def a2_out(d):
        part = a2.at[x, y]
        return remote(part, part, a2_send.at[d], a2_recv.at[d], sec, g * RUN + mate(d))

    def a2_in(d):
        part = a2.at[x, mate_in(d)]
        return remote(part, part, a2_send.at[d], a2_recv.at[d], sec, g * RUN + mate_in(d))

    def b2_out(d):
        return remote(a2.at[x], a2.at[x], b2_send.at[d], b2_recv.at[d], sec, across(beside(d)))

    def b2_in(d):
        part = a2.at[beside_in(d)]
        return remote(part, part, b2_send.at[d], b2_recv.at[d], sec, across(beside_in(d)))

    for d in range(1, GROUPS):
        rs_in(d).wait_recv()
    total = rsb[0].astype(F32)
    for d in range(1, GROUPS):
        total = total + rsb[d].astype(F32)
    final = total[TILES - 1]
    pair = split(final[:, 0:1] + final[:, 1:2])
    a1[y, x] = total[:AHEAD].astype(BF16)
    a2[x, y, 0:TILES - 1 - AHEAD] = total[AHEAD:TILES - 1].astype(BF16)
    a2[x, y, TILES - 1 - AHEAD] = jnp.where(x == WIDE - 1, pair, final).astype(BF16)
    for d in range(1, WIDE):
        a1_out(d).start()
    for d in range(1, RUN):
        a2_out(d).start()
    act_ref[...] = act6[2:4]
    for d in range(1, WIDE):
        a1_in(d).wait_recv()
    for d in range(1, RUN):
        b1_out(d).start()
    for d in range(1, RUN):
        a2_in(d).wait_recv()
    for d in range(1, WIDE):
        b2_out(d).start()

    @when(has_low)
    def _():
        halo(True).wait_send()

    @when(has_high)
    def _():
        halo(False).wait_send()

    for step in range(4):
        up_out(step).wait_send()
        if step < 3:
            down_out(step).wait_send()

    @when(odd)
    def _():
        for r in range(1, 5):
            to_sibling(r).wait_send()

    @when(sec >= 4, odd)
    def _():
        to_skip(4).wait_send()

    @when(sec >= 4, even)
    def _():
        to_skip(2).wait_send()

    for i in range(2):
        @when(has_end[i])
        def _():
            for d in range(1, RUN):
                end_out(i, d).wait_send()

    for d in range(1, RUN):
        mx_out(d).wait_send()
        rs_out(d).wait_send()
        a2_out(d).wait_send()
        b1_out(d).wait_send()
    for d in range(1, WIDE):
        a1_out(d).wait_send()
        b2_out(d).wait_send()
        b2_in(d).wait_recv()
    for d in range(1, RUN):
        b1_in(d).wait_recv()


def finish(norm_factor, act_in, a1, a2, act_ref, kg_ref, bias_ref):
    act_ref[0] = act_in[...].reshape(act_ref.shape[1:])
    for t in range(WIDE * TILES):
        q, i = t // TILES, t % TILES
        if i < AHEAD:
            tile = a1[:, q, i]
        else:
            tile = a2[q, :, i - AHEAD]
        tile = tile.reshape(128, 128).astype(F32).T * norm_factor
        if t < 27:
            kg_ref[0, t] = tile
        else:
            bias_ref[...] = tile[0:1] + tile[1:2]


def local(saved_in, saved_out, weights, cotangent):
    rows_y, cells_x, cells_z, channels = cotangent.shape
    norm_factor = 1.0 / math.sqrt(rows_y * lax.axis_size("slab") * cells_x * cells_z)
    flat = (rows_y, cells_x * cells_z, channels)
    vmem = pl.BlockSpec(memory_space=pltpu.VMEM)
    hbm = pl.BlockSpec(memory_space=pl.ANY)
    six = pltpu.VMEM((6, 256, 128), BF16)
    two = pltpu.VMEM((2, 256, 128), BF16)
    sems = pltpu.SemaphoreType.DMA
    act, a1, a2 = pl.pallas_call(
        kernel,
        name="backward",
        out_shape=(
            jax.ShapeDtypeStruct(flat, BF16),
            jax.ShapeDtypeStruct((RUN, WIDE, AHEAD, SHARE, channels), BF16),
            jax.ShapeDtypeStruct((WIDE, RUN, TILES - AHEAD, SHARE, channels), BF16),
        ),
        in_specs=[hbm] * 4,
        out_specs=(vmem,) * 3,
        scratch_shapes=[
            pltpu.VMEM((27, 128, 128), BF16), two, two,
            six, six, six, six,
            pltpu.VMEM((6, 256, 1152), BF16),
            pltpu.VMEM((1152, 384), BF16),
            pltpu.VMEM((RUN, SHARE, 512), BF16),
            pltpu.VMEM((RUN, SHARE, 256), BF16),
            pltpu.VMEM((RUN, SHARE, 512), BF16),
            pltpu.VMEM((2, SHARE, 256), BF16),
            pltpu.VMEM((9 * SHARE, RUN * 512 + 512), BF16),
            pltpu.VMEM((2 * RUN, 256, 128), BF16),
            pltpu.VMEM((WIDE, TILES, SHARE, 128), BF16),
            pltpu.VMEM((GROUPS, TILES, SHARE, 128), BF16),
            sems((4,)), sems((2,)), sems((2,)),
            sems((4,)), sems((4,)), sems((6,)), sems((6,)), sems, sems((2,)),
            pltpu.SemaphoreType.REGULAR,
            sems((4,)), sems((4,)), sems((3,)), sems((3,)), sems((8,)), sems((2,)),
            sems((8,)), sems((8,)), sems((8,)), sems((8,)),
            sems((8,)), sems((8,)), sems((8,)), sems((8,)),
            sems((8,)), sems((8,)), sems((8,)), sems((8,)),
        ],
        compiler_params=pltpu.CompilerParams(
            collective_id=0, has_side_effects=True, vmem_limit_bytes=56 << 20
        ),
    )(
        saved_in[0].reshape(flat), saved_out[0].reshape(flat), weights[0], cotangent.reshape(flat)
    )
    return pl.pallas_call(
        functools.partial(finish, norm_factor),
        name="finish",
        out_shape=(
            jax.ShapeDtypeStruct((1,) + cotangent.shape, BF16),
            jax.ShapeDtypeStruct((1, 27, channels, channels), F32),
            jax.ShapeDtypeStruct((1, channels), F32),
        ),
        in_specs=[vmem] * 3,
        out_specs=(vmem,) * 3,
    )(act, a1, a2)


def solution(mesh):
    placed = (
        P("section", "slab", None, None, None),
        P("section", "slab", None, None, None),
        P("section", None, None, None),
        P("slab", None, None, None),
    )
    return jax.shard_map(
        local,
        mesh=mesh,
        in_specs=placed,
        out_specs=(
            P("section", "slab", None, None, None),
            P("section", None, None, None),
            P("section", None),
        ),
        check_vma=False,
    )
```

```python
import functools
import math

import jax
import jax.numpy as jnp
from jax import lax
from jax.experimental import pallas as pl
from jax.experimental.pallas import tpu as pltpu
from jax.sharding import PartitionSpec as P

MESH = pl.DeviceIdType.MESH
F32 = jnp.float32
BF16 = jnp.bfloat16

RUN = 8
GROUPS = 8
SHARE = 16
WIDE = 4
TILES = 7
AHEAD = 2


def kernel(
    si_ref, so_ref, w_ref, cot_ref,
    act_ref, a1, a2,
    wv, sov, cotv, inc, so6, act6, skip6, s9, w9, sob, act6b, skip6b, s9b, w9b, mt, mtx, mrun, ends, lhs, srun, kgc, rsb,
    load, halo_send, halo_recv, row_send, row_recv, slab_send, slab_recv, skip_send, skip_recv,
    pair_send, pair_recv, skip_send_b, skip_recv_b, go,
    up_send, up_recv, down_send, down_recv, end_send, end_recv,
    mx_send, mx_recv, rs_send, rs_recv,
    a1_send, a1_recv, b1_send, b1_recv, a2_send, a2_recv, b2_send, b2_recv,
):
    sec = lax.axis_index("section")
    j = lax.axis_index("slab")
    n_sec = lax.axis_size("section")
    n_slab = lax.axis_size("slab")
    y = lax.rem(j, RUN)
    g = lax.div(j, RUN)
    odd = lax.rem(sec, 2) == 1
    even = lax.rem(sec, 2) == 0
    has_low = j > 0
    has_high = j < n_slab - 1
    top = sec == n_sec - 1
    first = y == 0
    last = y == RUN - 1
    x = lax.div(g, 2)
    high = lax.rem(g, 2)

    def both(*conditions):
        out = conditions[0]
        for c in conditions[1:]:
            out = jnp.logical_and(out, c)
        return out

    def when(*conditions):
        return pl.when(both(*conditions))

    def loads():
        return (
            pltpu.make_async_copy(so_ref, sov, load.at[0]),
            pltpu.make_async_copy(cot_ref, cotv, load.at[1]),
            pltpu.make_async_copy(w_ref, wv, load.at[2]),
            pltpu.make_async_copy(si_ref, srun.at[pl.ds(1 + 2 * y, 2)], load.at[3]),
        )

    for c in loads():
        c.start()

    barrier = pltpu.get_barrier_semaphore()

    def signal(s, t):
        pl.semaphore_signal(barrier, inc=1, device_id=(s, t), device_id_type=MESH)

    @when(has_low, first)
    def _():
        signal(sec, j - 1)

    @when(has_high, last)
    def _():
        signal(sec, j + 1)

    for d in range(1, RUN):
        signal(sec, g * RUN + lax.rem(y + d, RUN))
    for d in range(1, GROUPS):
        signal(sec, lax.rem(g + d, GROUPS) * RUN + y)

    @when(sec > 0)
    def _():
        signal(sec - 1, j)

    @when(jnp.logical_not(top))
    def _():
        signal(sec + 1, j)

    for step, there in ((-2, both(odd, sec > 1)), (2, both(odd, jnp.logical_not(top)))):
        @when(there)
        def _():
            signal(sec + step, j)

        @when(there, has_low)
        def _():
            signal(sec + step, j - 1)

        @when(there, has_high)
        def _():
            signal(sec + step, j + 1)

    @when(sec >= 4)
    def _():
        signal(sec - 4, j)

    @when(sec < 4)
    def _():
        signal(sec + 4, j)

    def one(*conditions):
        return jnp.where(both(*conditions), 1, 0)

    pairs = one(odd, sec > 1) + one(odd, jnp.logical_not(top))
    expected = (
        RUN - 1 + GROUPS - 1 + 1
        + one(has_low, first) + one(has_high, last)
        + one(sec > 0) + one(jnp.logical_not(top))
        + pairs * (1 + one(has_low) + one(has_high))
    )

    blank = jnp.zeros((2, 256, 128), BF16)

    @when(jnp.logical_not(has_low))
    def _():
        so6[0:2] = blank

        @when(odd)
        def _():
            inc[0:2] = blank

    @when(jnp.logical_not(has_high))
    def _():
        so6[4:6] = blank

        @when(odd)
        def _():
            inc[4:6] = blank

    srun[0] = blank[0]
    srun[2 * RUN + 1] = blank[0]

    @when(g == 0)
    def _():
        ends[0] = jnp.zeros((SHARE, 256), BF16)

    @when(g == GROUPS - 1)
    def _():
        ends[1] = jnp.zeros((SHARE, 256), BF16)

    load_so, load_cot, load_w, load_si = loads()
    load_so.wait()
    load_cot.wait()

    @when(top)
    def _():
        so6[2:4] = jnp.where(sov[...].astype(F32) > 0, cotv[...].astype(F32), 0.0).astype(BF16)

    @when(jnp.logical_not(top))
    def _():
        so6[2:4] = sov[...]

    load_si.wait()

    pl.semaphore_wait(barrier, expected)

    def remote(src, dst, ss, rs, s, t):
        return pltpu.make_async_remote_copy(
            src_ref=src, dst_ref=dst, send_sem=ss, recv_sem=rs,
            device_id=(s, t), device_id_type=MESH,
        )

    def halo(low):
        own = so6.at[2:4]
        if low:
            return remote(own, so6.at[4:6], halo_send.at[0], halo_recv.at[0], sec, j - 1)
        return remote(own, so6.at[0:2], halo_send.at[1], halo_recv.at[1], sec, j + 1)

    @when(has_low)
    def _():
        halo(True).start()

    @when(has_high)
    def _():
        halo(False).start()

    load_w.wait()

    def turn(k, carry):
        dy, dx, dz = lax.div(k, 9), lax.rem(lax.div(k, 3), 3), lax.rem(k, 3)
        tile = wv[k].astype(F32).T.astype(BF16)
        rows = pl.ds(pl.multiple_of(dx * 384 + dz * 128, 128), 128)
        w9[rows, pl.ds(pl.multiple_of(dy * 128, 128), 128)] = tile
        return carry

    lax.fori_loop(0, 27, turn, 0)
    def to_pair(i):
        if i == 0:
            return remote(w9, w9b, pair_send.at[0], pair_recv.at[0], sec + 1, j)
        return remote(so6.at[1:5], sob.at[1:5], pair_send.at[1], pair_recv.at[1], sec + 1, j)

    @when(even, sec > 0)
    def _():
        to_pair(0).start()

    def mate(d):
        return lax.rem(y + d, RUN)

    def mate_in(d):
        return lax.rem(y + RUN - d, RUN)

    def peer(d):
        return lax.rem(g + d, GROUPS)

    def peer_in(d):
        return lax.rem(g + GROUPS - d, GROUPS)

    def rows_of(origin):
        return srun.at[pl.ds(1 + 2 * origin, 2)]

    def up_out(step):
        rows = rows_of(lax.rem(y + RUN - step, RUN))
        return remote(rows, rows, up_send.at[step], up_recv.at[step], sec, g * RUN + mate(1))

    def up_in(step):
        rows = rows_of(lax.rem(y + RUN - step - 1, RUN))
        return remote(rows, rows, up_send.at[step], up_recv.at[step], sec, g * RUN + mate(1))

    def down_out(step):
        rows = rows_of(lax.rem(y + step, RUN))
        return remote(rows, rows, down_send.at[step], down_recv.at[step], sec, g * RUN + mate(RUN - 1))

    def down_in(step):
        rows = rows_of(lax.rem(y + step + 1, RUN))
        return remote(rows, rows, down_send.at[step], down_recv.at[step], sec, g * RUN + mate(RUN - 1))

    low_row = g > 0
    high_row = g < GROUPS - 1

    def gather_run(steps):
        for step in steps:
            up_out(step).start()
            if step < 3:
                down_out(step).start()
            up_in(step).wait_recv()
            if step < 3:
                down_in(step).wait_recv()

    def halo_wait(low):
        if low:
            @when(has_low)
            def _():
                halo(False).wait_recv()
        else:
            @when(has_high)
            def _():
                halo(True).wait_recv()

    @when(even)
    def _():
        halo_wait(True)
        halo_wait(False)

    @when(even, sec > 0)
    def _():
        to_pair(1).start()

    @when(sec < n_sec - 2)
    def _():
        gather_run((0, 1))

    @when(sec < n_sec // 2)
    def _():
        gather_run((2, 3))

    def to_sibling(r):
        return remote(act6.at[r], inc.at[r], row_send.at[r - 1], row_recv.at[r - 1], sec - 1, j)

    def to_slab(i, which):
        at = (2, 4, 0)[which] + i
        k = 3 * i + which
        return remote(
            act6b.at[2 + i], inc.at[at], slab_send.at[k], slab_recv.at[k], sec - 2, j + (0, -1, 1)[which]
        )

    def slab_sends(i, act):
        getattr(to_slab(i, 0), act)()

        @when(has_low)
        def _():
            getattr(to_slab(i, 1), act)()

        @when(has_high)
        def _():
            getattr(to_slab(i, 2), act)()

    def to_skip(rows):
        if rows == 4:
            return remote(act6.at[1:5], skip6.at[1:5], skip_send, skip_recv.at[0], sec - 4, j)
        return remote(act6.at[2:4], skip6.at[2:4], skip_send, skip_recv.at[1], sec - 4, j)

    def to_skip_b():
        return remote(act6b.at[2:4], skip6b.at[2:4], skip_send_b, skip_recv_b, sec - 4, j)

    depth = lax.broadcasted_iota(jnp.int32, (32, 8, 128), 1)
    edge_x = jnp.zeros((8, 128), F32)

    def stack_row(r, carry):
        held = so6[r].astype(F32)
        arrived = jnp.where(held > 0, inc[r].astype(F32), 0.0)
        put_row(s9, r, jnp.where(top, held, arrived))
        return carry

    def stack_pair(r, carry):
        put_row(s9b, r, jnp.where(sob[r].astype(F32) > 0, act6[r].astype(F32), 0.0))
        return carry

    def put_row(s9, r, m):
        m = m.reshape(32, 8, 128)
        up = jnp.where(depth == 7, 0.0, pltpu.roll(m, 7, 1)).reshape(256, 128)
        down = jnp.where(depth == 0, 0.0, pltpu.roll(m, 1, 1)).reshape(256, 128)
        for b, v in enumerate((up, m.reshape(256, 128), down)):
            at = b * 128
            s9[r, :, at:at + 128] = jnp.concatenate([v[8:], edge_x], 0).astype(BF16)
            s9[r, :, at + 384:at + 512] = v.astype(BF16)
            s9[r, :, at + 768:at + 896] = jnp.concatenate([edge_x, v[:-8]], 0).astype(BF16)

    mine = (s9, w9, skip6, act6)
    pair = (s9b, w9b, skip6b, act6b)

    def layer(refs, lo, hi, steps, done):
        s9, w9, skip6, act6 = refs
        sums, count = {}, {}
        for ready, rows in steps:
            ready()
            for t in rows:
                reach = [dy for dy in (-1, 0, 1) if lo <= t + dy < hi]
                p = jnp.dot(
                    s9[t], w9[:, (reach[0] + 1) * 128:(reach[-1] + 2) * 128],
                    preferred_element_type=F32,
                )
                for i, dy in enumerate(reach):
                    r = t + dy
                    v = p[:, i * 128:(i + 1) * 128]
                    sums[r] = sums[r] + v if r in sums else v
                    count[r] = count.get(r, 0) + 1
                    if count[r] == 3:
                        total = sums.pop(r)
                        total = jnp.where(sec < 4, total + skip6[r].astype(F32), total)
                        act6[r] = total.astype(BF16)
                        done(r)

    def odd_layer(low_first):
        def own():
            @when(jnp.logical_not(top))
            def _():
                to_slab(0, 0).wait_recv()
                to_slab(1, 0).wait_recv()

            lax.fori_loop(2, 4, stack_row, 0)

        def side(low):
            halo_wait(low)

            @when(jnp.logical_not(top), has_low if low else has_high)
            def _():
                for i in range(2):
                    to_slab(i, 2 if low else 1).wait_recv()

            at = 0 if low else 4
            lax.fori_loop(at, at + 2, stack_row, 0)

        @when(sec < 4)
        def _():
            to_skip(4).wait_recv()

        lows = (lambda: side(True), (0, 1))
        highs = (lambda: side(False), (4, 5))
        order = [lows, highs] if low_first else [highs, lows]
        layer(mine, 1, 5, [(own, (2, 3))] + order, lambda r: to_sibling(r).start())

        @when(sec > 1)
        def _():
            to_pair(0).wait_recv()
            to_pair(1).wait_recv()

            @when(sec < 4)
            def _():
                to_skip_b().wait_recv()

            rows = (1, 2, 3, 4) if low_first else (4, 3, 2, 1)
            layer(
                pair, 2, 4,
                [(lambda r=r: lax.fori_loop(r, r + 1, stack_pair, 0), (r,)) for r in rows],
                lambda r: slab_sends(r - 2, "start"),
            )

    def even_layer(low_first):
        rows = (1, 2, 3, 4) if low_first else (4, 3, 2, 1)

        def ready(r):
            to_sibling(r).wait_recv()
            lax.fori_loop(r, r + 1, stack_row, 0)

        @when(sec < 4)
        def _():
            to_skip(2).wait_recv()

        layer(mine, 2, 4, [(lambda r=r: ready(r), (r,)) for r in rows], lambda r: None)

    @when(odd, first)
    def _():
        odd_layer(False)

    @when(odd, jnp.logical_not(first))
    def _():
        odd_layer(True)

    @when(even, sec > 0, first)
    def _():
        even_layer(False)

    @when(even, sec > 0, jnp.logical_not(first))
    def _():
        even_layer(True)

    @when(sec == 0)
    def _():
        for r in (2, 3):
            to_sibling(r).wait_recv()
        lax.fori_loop(2, 4, stack_row, 0)

    def turned(r, h):
        block = s9[r, h * 128:(h + 1) * 128, 512:640].astype(F32).T.astype(BF16)
        return block.reshape(RUN, SHARE, 128)

    for r in range(2):
        for h in range(2):
            at = r * 256 + h * 128
            mt[:, :, at:at + 128] = turned(2 + r, h)

    @when(odd, sec > 1)
    def _():
        slab_sends(0, "wait_send")
        slab_sends(1, "wait_send")
        pl.semaphore_signal(go, inc=1, device_id=(sec - 1, j), device_id_type=MESH)

    @when(even, sec > 0)
    def _():
        pl.semaphore_wait(go, 1)

    @when(top)
    def _():
        to_skip_b().start()

    @when(sec >= 4, odd)
    def _():
        to_skip(4).start()

    @when(sec >= 4, even)
    def _():
        to_skip(2).start()

    def mx_out(d):
        return remote(mt.at[mate(d)], mrun.at[y], mx_send.at[d], mx_recv.at[d], sec, g * RUN + mate(d))

    def mx_in(d):
        return remote(mt.at[y], mrun.at[mate_in(d)], mx_send.at[d], mx_recv.at[d], sec, g * RUN + mate_in(d))

    def end_out(i, d):
        return remote(mtx.at[mate(d)], ends.at[i], end_send.at[d], end_recv.at[i], sec, g * RUN + mate(d))

    for d in range(1, RUN):
        mx_out(d).start()
    mrun[y] = mt[y]

    @when(sec == 0)
    def _():
        for r in (1, 4):
            to_sibling(r).wait_recv()
            lax.fori_loop(r, r + 1, stack_row, 0)

    for outer, r in ((both(first, low_row), 1), (both(last, high_row), 4)):
        @when(outer)
        def _():
            for h in range(2):
                mtx[:, :, h * 128:(h + 1) * 128] = turned(r, h)

    has_end = (both(first, low_row), both(last, high_row))
    for i in range(2):
        @when(has_end[i])
        def _():
            for d in range(1, RUN):
                end_out(i, d).start()
            ends[i] = mtx[y]

    @when(sec == 0)
    def _():
        to_skip(2).wait_recv()
        layer(mine, 2, 4, [(lambda: None, (1, 2, 3, 4))], lambda r: None)

    @when(sec >= n_sec - 2)
    def _():
        gather_run((0, 1))

    @when(sec >= n_sec // 2)
    def _():
        gather_run((2, 3))

    lane = lax.broadcasted_iota(jnp.int32, (SHARE, 512), 1)
    cell_x = lax.rem(lax.div(lane, 8), 32)
    cell_z = lax.rem(lane, 8)
    fits = []
    for dx in (-1, 0, 1):
        for dz in (-1, 0, 1):
            fits.append(both(cell_x - dx >= 0, cell_x - dx < 32, cell_z - dz >= 0, cell_z - dz < 8))

    def spread(m, slot, width):
        for i, ok in enumerate(fits):
            step = ((i // 3 - 1) * 8 + i % 3 - 1) % width
            moved = m if step == 0 else jnp.where(ok[:, :width], pltpu.roll(m, step, 1), 0.0)
            lhs[slot, i * SHARE:(i + 1) * SHARE, 0:width] = moved.astype(BF16)

    bias = jnp.zeros((SHARE, 512), F32)
    terms = [jnp.zeros((9 * SHARE, 128), F32)] * 3
    for n, d in enumerate((0, 1, 7, 2, 6, 3, 5, 4)):
        if d > 0:
            mx_in(d).wait_recv()
        u = mate_in(d)
        m = mrun[u].astype(F32)
        bias = bias + m
        spread(m, n, 512)
        for dy in range(3):
            terms[dy] = terms[dy] + jnp.dot(
                lhs[n], srun[pl.ds(2 * u + dy, 2)].reshape(512, 128), preferred_element_type=F32
            )
    for i, (there, away) in enumerate(((low_row, y > 0), (high_row, y < RUN - 1))):
        @when(there, away)
        def _():
            end_out(i, 1).wait_recv()

        spread(ends[i].astype(F32), RUN + i, 256)
        dy, row = ((2, 1), (0, 2 * RUN))[i]
        terms[dy] = terms[dy] + jnp.dot(
            lhs[RUN + i, :, 0:256], srun[row], preferred_element_type=F32
        )

    column = lax.broadcasted_iota(jnp.int32, (SHARE, 128), 1)

    def split(total):
        head = total.astype(BF16).astype(F32)
        return jnp.where(column == 0, head, jnp.where(column == 1, total - head, 0.0))

    for dy in range(3):
        block = terms[dy].astype(BF16)
        for i in range(9):
            t = dy * 9 + i
            kgc[t // TILES, t % TILES] = block[i * SHARE:(i + 1) * SHARE]
    kgc[WIDE - 1, TILES - 1] = split(jnp.sum(bias, axis=1, keepdims=True)).astype(BF16)

    def rs_out(d):
        return remote(
            kgc.at[lax.div(peer(d), 2)], rsb.at[g], rs_send.at[d], rs_recv.at[d], sec, peer(d) * RUN + y
        )

    def rs_in(d):
        return remote(
            kgc.at[0], rsb.at[peer_in(d)], rs_send.at[d], rs_recv.at[d], sec, peer_in(d) * RUN + y
        )

    for d in range(1, GROUPS):
        rs_out(d).start()
    rsb[g] = kgc[x]

    def beside(d):
        return lax.rem(x + d, WIDE)

    def beside_in(d):
        return lax.rem(x + WIDE - d, WIDE)

    def across(at):
        return (2 * at + high) * RUN + y

    def a1_out(d):
        part = a1.at[y, x]
        return remote(part, part, a1_send.at[d], a1_recv.at[d], sec, across(beside(d)))

    def a1_in(d):
        part = a1.at[y, beside_in(d)]
        return remote(part, part, a1_send.at[d], a1_recv.at[d], sec, across(beside_in(d)))

    def b1_out(d):
        return remote(a1.at[y], a1.at[y], b1_send.at[d], b1_recv.at[d], sec, g * RUN + mate(d))

    def b1_in(d):
        part = a1.at[mate_in(d)]
        return remote(part, part, b1_send.at[d], b1_recv.at[d], sec, g * RUN + mate_in(d))

    def a2_out(d):
        part = a2.at[x, y]
        return remote(part, part, a2_send.at[d], a2_recv.at[d], sec, g * RUN + mate(d))

    def a2_in(d):
        part = a2.at[x, mate_in(d)]
        return remote(part, part, a2_send.at[d], a2_recv.at[d], sec, g * RUN + mate_in(d))

    def b2_out(d):
        return remote(a2.at[x], a2.at[x], b2_send.at[d], b2_recv.at[d], sec, across(beside(d)))

    def b2_in(d):
        part = a2.at[beside_in(d)]
        return remote(part, part, b2_send.at[d], b2_recv.at[d], sec, across(beside_in(d)))

    for d in range(1, GROUPS):
        rs_in(d).wait_recv()
    total = rsb[0].astype(F32)
    for d in range(1, GROUPS):
        total = total + rsb[d].astype(F32)
    final = total[TILES - 1]
    pair = split(final[:, 0:1] + final[:, 1:2])
    a1[y, x] = total[:AHEAD].astype(BF16)
    a2[x, y, 0:TILES - 1 - AHEAD] = total[AHEAD:TILES - 1].astype(BF16)
    a2[x, y, TILES - 1 - AHEAD] = jnp.where(x == WIDE - 1, pair, final).astype(BF16)
    for d in range(1, WIDE):
        a1_out(d).start()
    for d in range(1, RUN):
        a2_out(d).start()
    act_ref[...] = act6[2:4]
    for d in range(1, WIDE):
        a1_in(d).wait_recv()
    for d in range(1, RUN):
        b1_out(d).start()
    for d in range(1, RUN):
        a2_in(d).wait_recv()
    for d in range(1, WIDE):
        b2_out(d).start()

    @when(has_low)
    def _():
        halo(True).wait_send()

    @when(has_high)
    def _():
        halo(False).wait_send()

    for step in range(4):
        up_out(step).wait_send()
        if step < 3:
            down_out(step).wait_send()

    @when(odd)
    def _():
        for r in range(1, 5):
            to_sibling(r).wait_send()

    @when(even, sec > 0)
    def _():
        to_pair(0).wait_send()
        to_pair(1).wait_send()

    @when(top)
    def _():
        to_skip_b().wait_send()

    @when(sec >= 4, odd)
    def _():
        to_skip(4).wait_send()

    @when(sec >= 4, even)
    def _():
        to_skip(2).wait_send()

    for i in range(2):
        @when(has_end[i])
        def _():
            for d in range(1, RUN):
                end_out(i, d).wait_send()

    for d in range(1, RUN):
        mx_out(d).wait_send()
        rs_out(d).wait_send()
        a2_out(d).wait_send()
        b1_out(d).wait_send()
    for d in range(1, WIDE):
        a1_out(d).wait_send()
        b2_out(d).wait_send()
        b2_in(d).wait_recv()
    for d in range(1, RUN):
        b1_in(d).wait_recv()


def finish(norm_factor, act_in, a1, a2, act_ref, kg_ref, bias_ref):
    act_ref[0] = act_in[...].reshape(act_ref.shape[1:])
    for t in range(WIDE * TILES):
        q, i = t // TILES, t % TILES
        tile = a1[:, q, i] if i < AHEAD else a2[q, :, i - AHEAD]
        tile = tile.reshape(128, 128).astype(F32).T * norm_factor
        if t < 27:
            kg_ref[0, t] = tile
        else:
            bias_ref[...] = tile[0:1] + tile[1:2]


def local(saved_in, saved_out, weights, cotangent):
    rows_y, cells_x, cells_z, channels = cotangent.shape
    norm_factor = 1.0 / math.sqrt(rows_y * lax.axis_size("slab") * cells_x * cells_z)
    flat = (rows_y, cells_x * cells_z, channels)
    vmem = pl.BlockSpec(memory_space=pltpu.VMEM)
    hbm = pl.BlockSpec(memory_space=pl.ANY)
    six = pltpu.VMEM((6, 256, 128), BF16)
    two = pltpu.VMEM((2, 256, 128), BF16)
    sems = pltpu.SemaphoreType.DMA
    act, a1, a2 = pl.pallas_call(
        kernel,
        name="backward",
        out_shape=(
            jax.ShapeDtypeStruct(flat, BF16),
            jax.ShapeDtypeStruct((RUN, WIDE, AHEAD, SHARE, channels), BF16),
            jax.ShapeDtypeStruct((WIDE, RUN, TILES - AHEAD, SHARE, channels), BF16),
        ),
        in_specs=[hbm] * 4,
        out_specs=(vmem,) * 3,
        scratch_shapes=[
            pltpu.VMEM((27, 128, 128), BF16), two, two,
            six, six, six, six,
            pltpu.VMEM((6, 256, 1152), BF16),
            pltpu.VMEM((1152, 384), BF16),
            six, six, six,
            pltpu.VMEM((6, 256, 1152), BF16),
            pltpu.VMEM((1152, 384), BF16),
            pltpu.VMEM((RUN, SHARE, 512), BF16),
            pltpu.VMEM((RUN, SHARE, 256), BF16),
            pltpu.VMEM((RUN, SHARE, 512), BF16),
            pltpu.VMEM((2, SHARE, 256), BF16),
            pltpu.VMEM((RUN + 2, 9 * SHARE, 512), BF16),
            pltpu.VMEM((2 * RUN + 2, 256, 128), BF16),
            pltpu.VMEM((WIDE, TILES, SHARE, 128), BF16),
            pltpu.VMEM((GROUPS, TILES, SHARE, 128), BF16),
            sems((4,)), sems((2,)), sems((2,)),
            sems((4,)), sems((4,)), sems((6,)), sems((6,)), sems, sems((2,)),
            sems((2,)), sems((2,)), sems, sems,
            pltpu.SemaphoreType.REGULAR,
            sems((4,)), sems((4,)), sems((3,)), sems((3,)), sems((8,)), sems((2,)),
            sems((8,)), sems((8,)), sems((8,)), sems((8,)),
            sems((8,)), sems((8,)), sems((8,)), sems((8,)),
            sems((8,)), sems((8,)), sems((8,)), sems((8,)),
        ],
        compiler_params=pltpu.CompilerParams(
            collective_id=0, has_side_effects=True, vmem_limit_bytes=56 << 20
        ),
    )(
        saved_in[0].reshape(flat), saved_out[0].reshape(flat), weights[0], cotangent.reshape(flat)
    )
    return pl.pallas_call(
        functools.partial(finish, norm_factor),
        name="finish",
        out_shape=(
            jax.ShapeDtypeStruct((1,) + cotangent.shape, BF16),
            jax.ShapeDtypeStruct((1, 27, channels, channels), F32),
            jax.ShapeDtypeStruct((1, channels), F32),
        ),
        in_specs=[vmem] * 3,
        out_specs=(vmem,) * 3,
    )(act, a1, a2)


def solution(mesh):
    placed = (
        P("section", "slab", None, None, None),
        P("section", "slab", None, None, None),
        P("section", None, None, None),
        P("slab", None, None, None),
    )
    return jax.shard_map(
        local,
        mesh=mesh,
        in_specs=placed,
        out_specs=(
            P("section", "slab", None, None, None),
            P("section", None, None, None),
            P("section", None),
        ),
        check_vma=False,
    )
```

```python
import functools
import math

import jax
import jax.numpy as jnp
from jax import lax
from jax.experimental import pallas as pl
from jax.experimental.pallas import tpu as pltpu
from jax.sharding import PartitionSpec as P

MESH = pl.DeviceIdType.MESH
F32 = jnp.float32
BF16 = jnp.bfloat16

RUN = 8
GROUPS = 8
SHARE = 16
WIDE = 4
TILES = 7
FAR = (4, 3, 5, 2, 6, 1, 7)
FAR_RUNS = (3, 5, 1, 7, 4, 2, 6)
AHEAD = 2


def kernel(
    si_ref, so_ref, w_ref, cot_ref,
    act_ref, a1, a2,
    wv, sov, cotv, inc, so6, act6, skip6, s9, w9, sob, act6b, skip6b, s9b, w9b, mt, mtx, mrun, ends, lhs, srun, kgc, rsb,
    load, halo_send, halo_recv, row_send, row_recv, slab_send, slab_recv, skip_send, skip_recv,
    pair_send, pair_recv, skip_send_b, skip_recv_b, go,
    up_send, up_recv, down_send, down_recv, end_send, end_recv,
    mx_send, mx_recv, rs_send, rs_recv,
    a1_send, a1_recv, b1_send, b1_recv, a2_send, a2_recv, b2_send, b2_recv,
):
    sec = lax.axis_index("section")
    j = lax.axis_index("slab")
    n_sec = lax.axis_size("section")
    n_slab = lax.axis_size("slab")
    y = lax.rem(j, RUN)
    g = lax.div(j, RUN)
    odd = lax.rem(sec, 2) == 1
    even = lax.rem(sec, 2) == 0
    has_low = j > 0
    has_high = j < n_slab - 1
    top = sec == n_sec - 1
    first = y == 0
    last = y == RUN - 1
    x = lax.div(g, 2)
    high = lax.rem(g, 2)

    def both(*conditions):
        out = conditions[0]
        for c in conditions[1:]:
            out = jnp.logical_and(out, c)
        return out

    def when(*conditions):
        return pl.when(both(*conditions))

    def loads():
        return (
            pltpu.make_async_copy(so_ref, sov, load.at[0]),
            pltpu.make_async_copy(cot_ref, cotv, load.at[1]),
            pltpu.make_async_copy(w_ref, wv, load.at[2]),
            pltpu.make_async_copy(si_ref, srun.at[pl.ds(1 + 2 * y, 2)], load.at[3]),
        )

    for c in loads():
        c.start()

    barrier = pltpu.get_barrier_semaphore()

    def signal(s, t):
        pl.semaphore_signal(barrier, inc=1, device_id=(s, t), device_id_type=MESH)

    @when(has_low, first)
    def _():
        signal(sec, j - 1)

    @when(has_high, last)
    def _():
        signal(sec, j + 1)

    for d in range(1, RUN):
        signal(sec, g * RUN + lax.rem(y + d, RUN))
    for d in range(1, GROUPS):
        signal(sec, lax.rem(g + d, GROUPS) * RUN + y)

    @when(sec > 0)
    def _():
        signal(sec - 1, j)

    @when(jnp.logical_not(top))
    def _():
        signal(sec + 1, j)

    for step, there in ((-2, both(odd, sec > 1)), (2, both(odd, jnp.logical_not(top)))):
        @when(there)
        def _():
            signal(sec + step, j)

        @when(there, has_low)
        def _():
            signal(sec + step, j - 1)

        @when(there, has_high)
        def _():
            signal(sec + step, j + 1)

    @when(sec >= 4)
    def _():
        signal(sec - 4, j)

    @when(sec < 4)
    def _():
        signal(sec + 4, j)

    def one(*conditions):
        return jnp.where(both(*conditions), 1, 0)

    pairs = one(odd, sec > 1) + one(odd, jnp.logical_not(top))
    expected = (
        RUN - 1 + GROUPS - 1 + 1
        + one(has_low, first) + one(has_high, last)
        + one(sec > 0) + one(jnp.logical_not(top))
        + pairs * (1 + one(has_low) + one(has_high))
    )

    blank = jnp.zeros((2, 256, 128), BF16)

    @when(jnp.logical_not(has_low))
    def _():
        so6[0:2] = blank

        @when(odd)
        def _():
            inc[0:2] = blank

    @when(jnp.logical_not(has_high))
    def _():
        so6[4:6] = blank

        @when(odd)
        def _():
            inc[4:6] = blank

    srun[0] = blank[0]
    srun[2 * RUN + 1] = blank[0]

    @when(g == 0)
    def _():
        ends[0] = jnp.zeros((SHARE, 256), BF16)

    @when(g == GROUPS - 1)
    def _():
        ends[1] = jnp.zeros((SHARE, 256), BF16)

    load_so, load_cot, load_w, load_si = loads()
    load_so.wait()
    load_cot.wait()

    @when(top)
    def _():
        so6[2:4] = jnp.where(sov[...].astype(F32) > 0, cotv[...].astype(F32), 0.0).astype(BF16)

    @when(jnp.logical_not(top))
    def _():
        so6[2:4] = sov[...]

    load_si.wait()

    pl.semaphore_wait(barrier, expected)

    def remote(src, dst, ss, rs, s, t):
        return pltpu.make_async_remote_copy(
            src_ref=src, dst_ref=dst, send_sem=ss, recv_sem=rs,
            device_id=(s, t), device_id_type=MESH,
        )

    def halo(low):
        own = so6.at[2:4]
        if low:
            return remote(own, so6.at[4:6], halo_send.at[0], halo_recv.at[0], sec, j - 1)
        return remote(own, so6.at[0:2], halo_send.at[1], halo_recv.at[1], sec, j + 1)

    @when(has_low)
    def _():
        halo(True).start()

    @when(has_high)
    def _():
        halo(False).start()

    load_w.wait()

    def turn(k, carry):
        dy, dx, dz = lax.div(k, 9), lax.rem(lax.div(k, 3), 3), lax.rem(k, 3)
        tile = wv[k].astype(F32).T.astype(BF16)
        rows = pl.ds(pl.multiple_of(dx * 384 + dz * 128, 128), 128)
        w9[rows, pl.ds(pl.multiple_of(dy * 128, 128), 128)] = tile
        return carry

    lax.fori_loop(0, 27, turn, 0)
    def to_pair(i):
        if i == 0:
            return remote(w9, w9b, pair_send.at[0], pair_recv.at[0], sec + 1, j)
        return remote(so6.at[1:5], sob.at[1:5], pair_send.at[1], pair_recv.at[1], sec + 1, j)

    @when(even, sec > 0)
    def _():
        to_pair(0).start()

    def mate(d):
        return lax.rem(y + d, RUN)

    def mate_in(d):
        return lax.rem(y + RUN - d, RUN)

    def peer(d):
        return lax.rem(g + d, GROUPS)

    def peer_in(d):
        return lax.rem(g + GROUPS - d, GROUPS)

    def rows_of(origin):
        return srun.at[pl.ds(1 + 2 * origin, 2)]

    def up_out(step):
        rows = rows_of(lax.rem(y + RUN - step, RUN))
        return remote(rows, rows, up_send.at[step], up_recv.at[step], sec, g * RUN + mate(1))

    def up_in(step):
        rows = rows_of(lax.rem(y + RUN - step - 1, RUN))
        return remote(rows, rows, up_send.at[step], up_recv.at[step], sec, g * RUN + mate(1))

    def down_out(step):
        rows = rows_of(lax.rem(y + step, RUN))
        return remote(rows, rows, down_send.at[step], down_recv.at[step], sec, g * RUN + mate(RUN - 1))

    def down_in(step):
        rows = rows_of(lax.rem(y + step + 1, RUN))
        return remote(rows, rows, down_send.at[step], down_recv.at[step], sec, g * RUN + mate(RUN - 1))

    low_row = g > 0
    high_row = g < GROUPS - 1

    def gather_run(steps):
        for step in steps:
            up_out(step).start()
            if step < 3:
                down_out(step).start()
            up_in(step).wait_recv()
            if step < 3:
                down_in(step).wait_recv()

    def halo_wait(low):
        if low:
            @when(has_low)
            def _():
                halo(False).wait_recv()
        else:
            @when(has_high)
            def _():
                halo(True).wait_recv()

    @when(even)
    def _():
        halo_wait(True)
        halo_wait(False)

    @when(even, sec > 0)
    def _():
        to_pair(1).start()

    @when(sec < n_sec - 2)
    def _():
        gather_run((0, 1))

    @when(sec < n_sec // 2)
    def _():
        gather_run((2, 3))

    def to_sibling(r):
        return remote(act6.at[r], inc.at[r], row_send.at[r - 1], row_recv.at[r - 1], sec - 1, j)

    def to_slab(i, which):
        at = (2, 4, 0)[which] + i
        k = 3 * i + which
        return remote(
            act6b.at[2 + i], inc.at[at], slab_send.at[k], slab_recv.at[k], sec - 2, j + (0, -1, 1)[which]
        )

    def slab_sends(i, act):
        getattr(to_slab(i, 0), act)()

        @when(has_low)
        def _():
            getattr(to_slab(i, 1), act)()

        @when(has_high)
        def _():
            getattr(to_slab(i, 2), act)()

    def to_skip(rows):
        if rows == 4:
            return remote(act6.at[1:5], skip6.at[1:5], skip_send, skip_recv.at[0], sec - 4, j)
        return remote(act6.at[2:4], skip6.at[2:4], skip_send, skip_recv.at[1], sec - 4, j)

    def to_skip_b():
        return remote(act6b.at[2:4], skip6b.at[2:4], skip_send_b, skip_recv_b, sec - 4, j)

    depth = lax.broadcasted_iota(jnp.int32, (32, 8, 128), 1)
    edge_x = jnp.zeros((8, 128), F32)

    def stack_row(r, carry):
        held = so6[r].astype(F32)
        arrived = jnp.where(held > 0, inc[r].astype(F32), 0.0)
        put_row(s9, r, jnp.where(top, held, arrived))
        return carry

    def stack_pair(r, carry):
        put_row(s9b, r, jnp.where(sob[r].astype(F32) > 0, act6[r].astype(F32), 0.0))
        return carry

    def put_row(s9, r, m):
        m = m.reshape(32, 8, 128)
        up = jnp.where(depth == 7, 0.0, pltpu.roll(m, 7, 1)).reshape(256, 128)
        down = jnp.where(depth == 0, 0.0, pltpu.roll(m, 1, 1)).reshape(256, 128)
        for b, v in enumerate((up, m.reshape(256, 128), down)):
            at = b * 128
            s9[r, :, at:at + 128] = jnp.concatenate([v[8:], edge_x], 0).astype(BF16)
            s9[r, :, at + 384:at + 512] = v.astype(BF16)
            s9[r, :, at + 768:at + 896] = jnp.concatenate([edge_x, v[:-8]], 0).astype(BF16)

    mine = (s9, w9, skip6, act6)
    pair = (s9b, w9b, skip6b, act6b)

    def layer(refs, lo, hi, steps, done):
        s9, w9, skip6, act6 = refs
        sums, count = {}, {}
        for ready, rows in steps:
            ready()
            for t in rows:
                reach = [dy for dy in (-1, 0, 1) if lo <= t + dy < hi]
                p = jnp.dot(
                    s9[t], w9[:, (reach[0] + 1) * 128:(reach[-1] + 2) * 128],
                    preferred_element_type=F32,
                )
                for i, dy in enumerate(reach):
                    r = t + dy
                    v = p[:, i * 128:(i + 1) * 128]
                    sums[r] = sums[r] + v if r in sums else v
                    count[r] = count.get(r, 0) + 1
                    if count[r] == 3:
                        total = sums.pop(r)
                        total = jnp.where(sec < 4, total + skip6[r].astype(F32), total)
                        act6[r] = total.astype(BF16)
                        done(r)

    def odd_layer(low_first):
        def own():
            @when(jnp.logical_not(top))
            def _():
                to_slab(0, 0).wait_recv()
                to_slab(1, 0).wait_recv()

            lax.fori_loop(2, 4, stack_row, 0)

        def side(low):
            halo_wait(low)

            @when(jnp.logical_not(top), has_low if low else has_high)
            def _():
                for i in range(2):
                    to_slab(i, 2 if low else 1).wait_recv()

            at = 0 if low else 4
            lax.fori_loop(at, at + 2, stack_row, 0)

        @when(sec < 4)
        def _():
            to_skip(4).wait_recv()

        lows = (lambda: side(True), (0, 1))
        highs = (lambda: side(False), (4, 5))
        order = [lows, highs] if low_first else [highs, lows]
        layer(mine, 1, 5, [(own, (2, 3))] + order, lambda r: to_sibling(r).start())

        @when(sec > 1)
        def _():
            to_pair(0).wait_recv()
            to_pair(1).wait_recv()

            @when(sec < 4)
            def _():
                to_skip_b().wait_recv()

            rows = (1, 2, 3, 4) if low_first else (4, 3, 2, 1)
            layer(
                pair, 2, 4,
                [(lambda r=r: lax.fori_loop(r, r + 1, stack_pair, 0), (r,)) for r in rows],
                lambda r: slab_sends(r - 2, "start"),
            )

    def even_layer(low_first):
        rows = (1, 2, 3, 4) if low_first else (4, 3, 2, 1)

        def ready(r):
            to_sibling(r).wait_recv()
            lax.fori_loop(r, r + 1, stack_row, 0)

        @when(sec < 4)
        def _():
            to_skip(2).wait_recv()

        layer(mine, 2, 4, [(lambda r=r: ready(r), (r,)) for r in rows], lambda r: None)

    @when(odd, first)
    def _():
        odd_layer(False)

    @when(odd, jnp.logical_not(first))
    def _():
        odd_layer(True)

    @when(even, sec > 0, first)
    def _():
        even_layer(False)

    @when(even, sec > 0, jnp.logical_not(first))
    def _():
        even_layer(True)

    @when(sec == 0)
    def _():
        for r in (2, 3):
            to_sibling(r).wait_recv()
        lax.fori_loop(2, 4, stack_row, 0)

    def turned(r, h):
        block = s9[r, h * 128:(h + 1) * 128, 512:640].astype(F32).T.astype(BF16)
        return block.reshape(RUN, SHARE, 128)

    for r in range(2):
        for h in range(2):
            at = r * 256 + h * 128
            mt[:, :, at:at + 128] = turned(2 + r, h)

    @when(odd, sec > 1)
    def _():
        slab_sends(0, "wait_send")
        slab_sends(1, "wait_send")
        pl.semaphore_signal(go, inc=1, device_id=(sec - 1, j), device_id_type=MESH)

    @when(even, sec > 0)
    def _():
        pl.semaphore_wait(go, 1)

    @when(top)
    def _():
        to_skip_b().start()

    @when(sec >= 4, odd)
    def _():
        to_skip(4).start()

    @when(sec >= 4, even)
    def _():
        to_skip(2).start()

    def mx_out(d):
        return remote(mt.at[mate(d)], mrun.at[y], mx_send.at[d], mx_recv.at[d], sec, g * RUN + mate(d))

    def mx_in(d):
        return remote(mt.at[y], mrun.at[mate_in(d)], mx_send.at[d], mx_recv.at[d], sec, g * RUN + mate_in(d))

    def end_out(i, d):
        return remote(mtx.at[mate(d)], ends.at[i], end_send.at[d], end_recv.at[i], sec, g * RUN + mate(d))

    for d in FAR:
        mx_out(d).start()
    mrun[y] = mt[y]

    @when(sec == 0)
    def _():
        for r in (1, 4):
            to_sibling(r).wait_recv()
            lax.fori_loop(r, r + 1, stack_row, 0)

    for outer, r in ((both(first, low_row), 1), (both(last, high_row), 4)):
        @when(outer)
        def _():
            for h in range(2):
                mtx[:, :, h * 128:(h + 1) * 128] = turned(r, h)

    has_end = (both(first, low_row), both(last, high_row))
    for i in range(2):
        @when(has_end[i])
        def _():
            for d in range(1, RUN):
                end_out(i, d).start()
            ends[i] = mtx[y]

    @when(sec >= n_sec - 2)
    def _():
        gather_run((0, 1))

    @when(sec >= n_sec // 2)
    def _():
        gather_run((2, 3))

    lane = lax.broadcasted_iota(jnp.int32, (SHARE, 512), 1)
    cell_x = lax.rem(lax.div(lane, 8), 32)
    cell_z = lax.rem(lane, 8)
    fits = []
    for dx in (-1, 0, 1):
        for dz in (-1, 0, 1):
            fits.append(both(cell_x - dx >= 0, cell_x - dx < 32, cell_z - dz >= 0, cell_z - dz < 8))

    def spread(m, slot, width):
        for i, ok in enumerate(fits):
            step = ((i // 3 - 1) * 8 + i % 3 - 1) % width
            moved = m if step == 0 else jnp.where(ok[:, :width], pltpu.roll(m, step, 1), 0.0)
            lhs[slot, i * SHARE:(i + 1) * SHARE, 0:width] = moved.astype(BF16)

    bias = jnp.zeros((SHARE, 512), F32)
    terms = [jnp.zeros((9 * SHARE, 128), F32)] * 3
    for n, d in enumerate((0, 1, 7, 2, 6, 3, 5, 4)):
        if d > 0:
            mx_in(d).wait_recv()
        u = mate_in(d)
        m = mrun[u].astype(F32)
        bias = bias + m
        spread(m, n, 512)
        for dy in range(3):
            terms[dy] = terms[dy] + jnp.dot(
                lhs[n], srun[pl.ds(2 * u + dy, 2)].reshape(512, 128), preferred_element_type=F32
            )
    for i, (there, away) in enumerate(((low_row, y > 0), (high_row, y < RUN - 1))):
        @when(there, away)
        def _():
            end_out(i, 1).wait_recv()

        spread(ends[i].astype(F32), RUN + i, 256)
        dy, row = ((2, 1), (0, 2 * RUN))[i]
        terms[dy] = terms[dy] + jnp.dot(
            lhs[RUN + i, :, 0:256], srun[row], preferred_element_type=F32
        )

    column = lax.broadcasted_iota(jnp.int32, (SHARE, 128), 1)

    def split(total):
        head = total.astype(BF16).astype(F32)
        return jnp.where(column == 0, head, jnp.where(column == 1, total - head, 0.0))

    for dy in range(3):
        block = terms[dy].astype(BF16)
        for i in range(9):
            t = dy * 9 + i
            kgc[t // TILES, t % TILES] = block[i * SHARE:(i + 1) * SHARE]
    kgc[WIDE - 1, TILES - 1] = split(jnp.sum(bias, axis=1, keepdims=True)).astype(BF16)

    def rs_out(d):
        return remote(
            kgc.at[lax.div(peer(d), 2)], rsb.at[g], rs_send.at[d], rs_recv.at[d], sec, peer(d) * RUN + y
        )

    def rs_in(d):
        return remote(
            kgc.at[0], rsb.at[peer_in(d)], rs_send.at[d], rs_recv.at[d], sec, peer_in(d) * RUN + y
        )

    for d in FAR_RUNS:
        rs_out(d).start()
    rsb[g] = kgc[x]

    @when(sec == 0)
    def _():
        to_skip(2).wait_recv()
        layer(mine, 2, 4, [(lambda: None, (1, 2, 3, 4))], lambda r: None)

    def beside(d):
        return lax.rem(x + d, WIDE)

    def beside_in(d):
        return lax.rem(x + WIDE - d, WIDE)

    def across(at):
        return (2 * at + high) * RUN + y

    def a1_out(d):
        part = a1.at[y, x]
        return remote(part, part, a1_send.at[d], a1_recv.at[d], sec, across(beside(d)))

    def a1_in(d):
        part = a1.at[y, beside_in(d)]
        return remote(part, part, a1_send.at[d], a1_recv.at[d], sec, across(beside_in(d)))

    def b1_out(d):
        return remote(a1.at[y], a1.at[y], b1_send.at[d], b1_recv.at[d], sec, g * RUN + mate(d))

    def b1_in(d):
        part = a1.at[mate_in(d)]
        return remote(part, part, b1_send.at[d], b1_recv.at[d], sec, g * RUN + mate_in(d))

    def a2_out(d):
        part = a2.at[x, y]
        return remote(part, part, a2_send.at[d], a2_recv.at[d], sec, g * RUN + mate(d))

    def a2_in(d):
        part = a2.at[x, mate_in(d)]
        return remote(part, part, a2_send.at[d], a2_recv.at[d], sec, g * RUN + mate_in(d))

    def b2_out(d):
        return remote(a2.at[x], a2.at[x], b2_send.at[d], b2_recv.at[d], sec, across(beside(d)))

    def b2_in(d):
        part = a2.at[beside_in(d)]
        return remote(part, part, b2_send.at[d], b2_recv.at[d], sec, across(beside_in(d)))

    for d in range(1, GROUPS):
        rs_in(d).wait_recv()
    total = rsb[0].astype(F32)
    for d in range(1, GROUPS):
        total = total + rsb[d].astype(F32)
    final = total[TILES - 1]
    pair = split(final[:, 0:1] + final[:, 1:2])
    a1[y, x] = total[:AHEAD].astype(BF16)
    a2[x, y, 0:TILES - 1 - AHEAD] = total[AHEAD:TILES - 1].astype(BF16)
    a2[x, y, TILES - 1 - AHEAD] = jnp.where(x == WIDE - 1, pair, final).astype(BF16)
    for d in range(1, WIDE):
        a1_out(d).start()
    for d in FAR:
        a2_out(d).start()
    act_ref[...] = act6[2:4].reshape(act_ref.shape)
    for d in range(1, WIDE):
        a1_in(d).wait_recv()
    for d in FAR:
        b1_out(d).start()
    for d in range(1, RUN):
        a2_in(d).wait_recv()
    for d in range(1, WIDE):
        b2_out(d).start()

    @when(has_low)
    def _():
        halo(True).wait_send()

    @when(has_high)
    def _():
        halo(False).wait_send()

    for step in range(4):
        up_out(step).wait_send()
        if step < 3:
            down_out(step).wait_send()

    @when(odd)
    def _():
        for r in range(1, 5):
            to_sibling(r).wait_send()

    @when(even, sec > 0)
    def _():
        to_pair(0).wait_send()
        to_pair(1).wait_send()

    @when(top)
    def _():
        to_skip_b().wait_send()

    @when(sec >= 4, odd)
    def _():
        to_skip(4).wait_send()

    @when(sec >= 4, even)
    def _():
        to_skip(2).wait_send()

    for i in range(2):
        @when(has_end[i])
        def _():
            for d in range(1, RUN):
                end_out(i, d).wait_send()

    for d in range(1, RUN):
        mx_out(d).wait_send()
        rs_out(d).wait_send()
        a2_out(d).wait_send()
        b1_out(d).wait_send()
    for d in range(1, WIDE):
        a1_out(d).wait_send()
        b2_out(d).wait_send()
        b2_in(d).wait_recv()
    for d in range(1, RUN):
        b1_in(d).wait_recv()


def finish(norm_factor, act_in, a1, a2, act_ref, kg_ref, bias_ref):
    act_ref[...] = act_in[...]
    for t in range(WIDE * TILES):
        q, i = t // TILES, t % TILES
        tile = a1[:, q, i] if i < AHEAD else a2[q, :, i - AHEAD]
        tile = tile.reshape(128, 128).astype(F32).T * norm_factor
        if t < 27:
            kg_ref[0, t] = tile
        else:
            bias_ref[...] = tile[0:1] + tile[1:2]


def local(saved_in, saved_out, weights, cotangent):
    rows_y, cells_x, cells_z, channels = cotangent.shape
    norm_factor = 1.0 / math.sqrt(rows_y * lax.axis_size("slab") * cells_x * cells_z)
    flat = (rows_y, cells_x * cells_z, channels)
    vmem = pl.BlockSpec(memory_space=pltpu.VMEM)
    hbm = pl.BlockSpec(memory_space=pl.ANY)
    six = pltpu.VMEM((6, 256, 128), BF16)
    two = pltpu.VMEM((2, 256, 128), BF16)
    sems = pltpu.SemaphoreType.DMA
    act, a1, a2 = pl.pallas_call(
        kernel,
        name="backward",
        out_shape=(
            jax.ShapeDtypeStruct((1,) + cotangent.shape, BF16),
            jax.ShapeDtypeStruct((RUN, WIDE, AHEAD, SHARE, channels), BF16),
            jax.ShapeDtypeStruct((WIDE, RUN, TILES - AHEAD, SHARE, channels), BF16),
        ),
        in_specs=[hbm] * 4,
        out_specs=(vmem,) * 3,
        scratch_shapes=[
            pltpu.VMEM((27, 128, 128), BF16), two, two,
            six, six, six, six,
            pltpu.VMEM((6, 256, 1152), BF16),
            pltpu.VMEM((1152, 384), BF16),
            six, six, six,
            pltpu.VMEM((6, 256, 1152), BF16),
            pltpu.VMEM((1152, 384), BF16),
            pltpu.VMEM((RUN, SHARE, 512), BF16),
            pltpu.VMEM((RUN, SHARE, 256), BF16),
            pltpu.VMEM((RUN, SHARE, 512), BF16),
            pltpu.VMEM((2, SHARE, 256), BF16),
            pltpu.VMEM((RUN + 2, 9 * SHARE, 512), BF16),
            pltpu.VMEM((2 * RUN + 2, 256, 128), BF16),
            pltpu.VMEM((WIDE, TILES, SHARE, 128), BF16),
            pltpu.VMEM((GROUPS, TILES, SHARE, 128), BF16),
            sems((4,)), sems((2,)), sems((2,)),
            sems((4,)), sems((4,)), sems((6,)), sems((6,)), sems, sems((2,)),
            sems((2,)), sems((2,)), sems, sems,
            pltpu.SemaphoreType.REGULAR,
            sems((4,)), sems((4,)), sems((3,)), sems((3,)), sems((8,)), sems((2,)),
            sems((8,)), sems((8,)), sems((8,)), sems((8,)),
            sems((8,)), sems((8,)), sems((8,)), sems((8,)),
            sems((8,)), sems((8,)), sems((8,)), sems((8,)),
        ],
        compiler_params=pltpu.CompilerParams(
            collective_id=0, has_side_effects=True, vmem_limit_bytes=56 << 20
        ),
    )(
        saved_in[0].reshape(flat), saved_out[0].reshape(flat), weights[0], cotangent.reshape(flat)
    )
    return pl.pallas_call(
        functools.partial(finish, norm_factor),
        name="finish",
        out_shape=(
            jax.ShapeDtypeStruct((1,) + cotangent.shape, BF16),
            jax.ShapeDtypeStruct((1, 27, channels, channels), F32),
            jax.ShapeDtypeStruct((1, channels), F32),
        ),
        in_specs=[vmem] * 3,
        out_specs=(vmem,) * 3,
    )(act, a1, a2)


def solution(mesh):
    placed = (
        P("section", "slab", None, None, None),
        P("section", "slab", None, None, None),
        P("section", None, None, None),
        P("slab", None, None, None),
    )
    return jax.shard_map(
        local,
        mesh=mesh,
        in_specs=placed,
        out_specs=(
            P("section", "slab", None, None, None),
            P("section", None, None, None),
            P("section", None),
        ),
        check_vma=False,
    )
```

```python
import functools
import math

import jax
import jax.numpy as jnp
from jax import lax
from jax.experimental import pallas as pl
from jax.experimental.pallas import tpu as pltpu
from jax.sharding import PartitionSpec as P

MESH = pl.DeviceIdType.MESH
F32 = jnp.float32
BF16 = jnp.bfloat16

RUN = 8
GROUPS = 8
SHARE = 16
WIDE = 4
TILES = 7
FAR = (4, 3, 5, 2, 6, 1, 7)
FAR_RUNS = (3, 5, 1, 7, 4, 2, 6)
AHEAD = 2


def kernel(
    si_ref, so_ref, w_ref, cot_ref,
    act_ref, a1, a2,
    wv, sov, cotv, inc, so6, act6, skip6, s9, w9, sob, act6b, skip6b, s9b, w9b, mt, mtx, mrun, ends, lhs, srun, kgc, rsb,
    load, halo_send, halo_recv, row_send, row_recv, slab_send, slab_recv, skip_send, skip_recv,
    pair_send, pair_recv, skip_send_b, skip_recv_b, go,
    up_send, up_recv, down_send, down_recv, end_send, end_recv,
    mx_send, mx_recv, rs_send, rs_recv,
    a1_send, a1_recv, b1_send, b1_recv, a2_send, a2_recv, b2_send, b2_recv,
):
    sec = lax.axis_index("section")
    j = lax.axis_index("slab")
    n_sec = lax.axis_size("section")
    n_slab = lax.axis_size("slab")
    y = lax.rem(j, RUN)
    g = lax.div(j, RUN)
    odd = lax.rem(sec, 2) == 1
    even = lax.rem(sec, 2) == 0
    has_low = j > 0
    has_high = j < n_slab - 1
    top = sec == n_sec - 1
    first = y == 0
    last = y == RUN - 1
    x = lax.div(g, 2)
    high = lax.rem(g, 2)

    def both(*conditions):
        out = jnp.bool_(conditions[0]) if conditions[0] is True else conditions[0]
        for c in conditions[1:]:
            out = jnp.logical_and(out, c)
        return out

    def when(*conditions):
        return pl.when(both(*conditions))

    def loads():
        return (
            pltpu.make_async_copy(so_ref, sov, load.at[0]),
            pltpu.make_async_copy(cot_ref, cotv, load.at[1]),
            pltpu.make_async_copy(w_ref, wv, load.at[2]),
            pltpu.make_async_copy(si_ref, srun.at[pl.ds(1 + 2 * y, 2)], load.at[3]),
        )

    for c in loads():
        c.start()

    barrier = pltpu.get_barrier_semaphore()

    def signal(s, t):
        pl.semaphore_signal(barrier, inc=1, device_id=(s, t), device_id_type=MESH)

    @when(has_low, first)
    def _():
        signal(sec, j - 1)

    @when(has_high, last)
    def _():
        signal(sec, j + 1)

    for d in range(1, RUN):
        signal(sec, g * RUN + lax.rem(y + d, RUN))
    for d in range(1, GROUPS):
        signal(sec, lax.rem(g + d, GROUPS) * RUN + y)

    @when(sec > 0)
    def _():
        signal(sec - 1, j)

    @when(jnp.logical_not(top))
    def _():
        signal(sec + 1, j)

    for step, there in ((-2, both(odd, sec > 1)), (2, both(odd, jnp.logical_not(top)))):
        @when(there)
        def _():
            signal(sec + step, j)

        @when(there, has_low)
        def _():
            signal(sec + step, j - 1)

        @when(there, has_high)
        def _():
            signal(sec + step, j + 1)

    @when(sec >= 4)
    def _():
        signal(sec - 4, j)

    @when(sec < 4)
    def _():
        signal(sec + 4, j)

    def one(*conditions):
        return jnp.where(both(*conditions), 1, 0)

    pairs = one(odd, sec > 1) + one(odd, jnp.logical_not(top))
    expected = (
        RUN - 1 + GROUPS - 1 + 1
        + one(has_low, first) + one(has_high, last)
        + one(sec > 0) + one(jnp.logical_not(top))
        + pairs * (1 + one(has_low) + one(has_high))
    )

    blank = jnp.zeros((2, 256, 128), BF16)

    @when(jnp.logical_not(has_low))
    def _():
        so6[0:2] = blank

        @when(odd)
        def _():
            inc[0:2] = blank

    @when(jnp.logical_not(has_high))
    def _():
        so6[4:6] = blank

        @when(odd)
        def _():
            inc[4:6] = blank

    srun[0] = blank[0]
    srun[2 * RUN + 1] = blank[0]

    @when(g == 0)
    def _():
        ends[0] = jnp.zeros((SHARE, 256), BF16)

    @when(g == GROUPS - 1)
    def _():
        ends[1] = jnp.zeros((SHARE, 256), BF16)

    load_so, load_cot, load_w, load_si = loads()
    load_so.wait()
    load_cot.wait()

    @when(top)
    def _():
        so6[2:4] = jnp.where(sov[...].astype(F32) > 0, cotv[...].astype(F32), 0.0).astype(BF16)

    @when(jnp.logical_not(top))
    def _():
        so6[2:4] = sov[...]

    load_si.wait()

    pl.semaphore_wait(barrier, expected)

    def remote(src, dst, ss, rs, s, t):
        return pltpu.make_async_remote_copy(
            src_ref=src, dst_ref=dst, send_sem=ss, recv_sem=rs,
            device_id=(s, t), device_id_type=MESH,
        )

    def halo(low, rows):
        if low:
            here, there = ((pl.ds(2, 2), pl.ds(4, 2)), (2, 4))[2 - rows]
        else:
            here, there = ((pl.ds(2, 2), pl.ds(0, 2)), (3, 1))[2 - rows]
        i = 0 if low else 1
        return remote(
            so6.at[here], so6.at[there], halo_send.at[i], halo_recv.at[i], sec, j - 1 if low else j + 1
        )

    def halo_do(low, there, act):
        for rows, parity in ((2, odd), (1, even)):
            @when(there, parity)
            def _():
                getattr(halo(low, rows), act)()

    halo_do(True, has_low, "start")
    halo_do(False, has_high, "start")

    load_w.wait()

    def turn(k, carry):
        dy, dx, dz = lax.div(k, 9), lax.rem(lax.div(k, 3), 3), lax.rem(k, 3)
        tile = wv[k].astype(F32).T.astype(BF16)
        rows = pl.ds(pl.multiple_of(dx * 384 + dz * 128, 128), 128)
        w9[rows, pl.ds(pl.multiple_of(dy * 128, 128), 128)] = tile
        return carry

    lax.fori_loop(0, 27, turn, 0)
    def to_pair(i):
        if i == 0:
            return remote(w9, w9b, pair_send.at[0], pair_recv.at[0], sec + 1, j)
        return remote(so6.at[1:5], sob.at[1:5], pair_send.at[1], pair_recv.at[1], sec + 1, j)

    @when(even, sec > 0)
    def _():
        to_pair(0).start()

    def mate(d):
        return lax.rem(y + d, RUN)

    def mate_in(d):
        return lax.rem(y + RUN - d, RUN)

    def peer(d):
        return lax.rem(g + d, GROUPS)

    def peer_in(d):
        return lax.rem(g + GROUPS - d, GROUPS)

    def rows_of(origin):
        return srun.at[pl.ds(1 + 2 * origin, 2)]

    def up_out(step):
        rows = rows_of(lax.rem(y + RUN - step, RUN))
        return remote(rows, rows, up_send.at[step], up_recv.at[step], sec, g * RUN + mate(1))

    def up_in(step):
        rows = rows_of(lax.rem(y + RUN - step - 1, RUN))
        return remote(rows, rows, up_send.at[step], up_recv.at[step], sec, g * RUN + mate(1))

    def down_out(step):
        rows = rows_of(lax.rem(y + step, RUN))
        return remote(rows, rows, down_send.at[step], down_recv.at[step], sec, g * RUN + mate(RUN - 1))

    def down_in(step):
        rows = rows_of(lax.rem(y + step + 1, RUN))
        return remote(rows, rows, down_send.at[step], down_recv.at[step], sec, g * RUN + mate(RUN - 1))

    low_row = g > 0
    high_row = g < GROUPS - 1

    def gather_run(steps):
        for step in steps:
            up_out(step).start()
            if step < 3:
                down_out(step).start()
            up_in(step).wait_recv()
            if step < 3:
                down_in(step).wait_recv()

    def halo_wait(low):
        halo_do(not low, has_low if low else has_high, "wait_recv")

    @when(even)
    def _():
        halo_wait(True)
        halo_wait(False)

    @when(even, sec > 0)
    def _():
        to_pair(1).start()

    @when(sec < n_sec - 2)
    def _():
        gather_run((0, 1))

    @when(sec < n_sec // 2)
    def _():
        gather_run((2, 3))

    def to_sibling(r):
        return remote(act6.at[r], inc.at[r], row_send.at[r - 1], row_recv.at[r - 1], sec - 1, j)

    def to_slab(i, which):
        at = (2, 4, 0)[which] + i
        k = 3 * i + which
        return remote(
            act6b.at[2 + i], inc.at[at], slab_send.at[k], slab_recv.at[k], sec - 2, j + (0, -1, 1)[which]
        )

    def slab_sends(i, act, order=(1, 2, 0)):
        for which in order:
            @when((True, has_low, has_high)[which])
            def _():
                getattr(to_slab(i, which), act)()

    def to_skip(rows):
        if rows == 4:
            return remote(act6.at[1:5], skip6.at[1:5], skip_send, skip_recv.at[0], sec - 4, j)
        return remote(act6.at[2:4], skip6.at[2:4], skip_send, skip_recv.at[1], sec - 4, j)

    def to_skip_b():
        return remote(act6b.at[2:4], skip6b.at[2:4], skip_send_b, skip_recv_b, sec - 4, j)

    depth = lax.broadcasted_iota(jnp.int32, (32, 8, 128), 1)
    edge_x = jnp.zeros((8, 128), F32)

    def stack_row(r, carry):
        held = so6[r].astype(F32)
        arrived = jnp.where(held > 0, inc[r].astype(F32), 0.0)
        put_row(s9, r, jnp.where(top, held, arrived))
        return carry

    def stack_pair(r, carry):
        put_row(s9b, r, jnp.where(sob[r].astype(F32) > 0, act6[r].astype(F32), 0.0))
        return carry

    def put_row(s9, r, m):
        m = m.reshape(32, 8, 128)
        up = jnp.where(depth == 7, 0.0, pltpu.roll(m, 7, 1)).reshape(256, 128)
        down = jnp.where(depth == 0, 0.0, pltpu.roll(m, 1, 1)).reshape(256, 128)
        for b, v in enumerate((up, m.reshape(256, 128), down)):
            at = b * 128
            s9[r, :, at:at + 128] = jnp.concatenate([v[8:], edge_x], 0).astype(BF16)
            s9[r, :, at + 384:at + 512] = v.astype(BF16)
            s9[r, :, at + 768:at + 896] = jnp.concatenate([edge_x, v[:-8]], 0).astype(BF16)

    mine = (s9, w9, skip6, act6)
    pair = (s9b, w9b, skip6b, act6b)

    def layer(refs, lo, hi, steps, done):
        s9, w9, skip6, act6 = refs
        sums, count = {}, {}
        for ready, rows in steps:
            ready()
            for t in rows:
                reach = [dy for dy in (-1, 0, 1) if lo <= t + dy < hi]
                p = jnp.dot(
                    s9[t], w9[:, (reach[0] + 1) * 128:(reach[-1] + 2) * 128],
                    preferred_element_type=F32,
                )
                for i, dy in enumerate(reach):
                    r = t + dy
                    v = p[:, i * 128:(i + 1) * 128]
                    sums[r] = sums[r] + v if r in sums else v
                    count[r] = count.get(r, 0) + 1
                    if count[r] == 3:
                        total = sums.pop(r)
                        total = jnp.where(sec < 4, total + skip6[r].astype(F32), total)
                        act6[r] = total.astype(BF16)
                        done(r)

    def odd_layer(low_first):
        def own():
            @when(jnp.logical_not(top))
            def _():
                to_slab(0, 0).wait_recv()
                to_slab(1, 0).wait_recv()

            lax.fori_loop(2, 4, stack_row, 0)

        def side(low):
            halo_wait(low)

            @when(jnp.logical_not(top), has_low if low else has_high)
            def _():
                for i in range(2):
                    to_slab(i, 2 if low else 1).wait_recv()

            at = 0 if low else 4
            lax.fori_loop(at, at + 2, stack_row, 0)

        @when(sec < 4)
        def _():
            to_skip(4).wait_recv()

        lows = (lambda: side(True), (0, 1))
        highs = (lambda: side(False), (4, 5))
        order = [lows, highs] if low_first else [highs, lows]
        layer(mine, 1, 5, [(own, (2, 3))] + order, lambda r: to_sibling(r).start())

        @when(sec > 1)
        def _():
            to_pair(0).wait_recv()
            to_pair(1).wait_recv()

            @when(sec < 4)
            def _():
                to_skip_b().wait_recv()

            rows = (1, 2, 3, 4) if low_first else (4, 3, 2, 1)
            layer(
                pair, 2, 4,
                [(lambda r=r: lax.fori_loop(r, r + 1, stack_pair, 0), (r,)) for r in rows],
                lambda r: slab_sends(r - 2, "start", (2, 1, 0) if low_first else (1, 2, 0)),
            )

    def even_layer(low_first):
        rows = (1, 2, 3, 4) if low_first else (4, 3, 2, 1)

        def ready(r):
            to_sibling(r).wait_recv()
            lax.fori_loop(r, r + 1, stack_row, 0)

        @when(sec < 4)
        def _():
            to_skip(2).wait_recv()

        layer(mine, 2, 4, [(lambda r=r: ready(r), (r,)) for r in rows], lambda r: None)

    @when(odd, first)
    def _():
        odd_layer(False)

    @when(odd, jnp.logical_not(first))
    def _():
        odd_layer(True)

    @when(even, sec > 0, first)
    def _():
        even_layer(False)

    @when(even, sec > 0, jnp.logical_not(first))
    def _():
        even_layer(True)

    @when(sec == 0)
    def _():
        for r in (2, 3):
            to_sibling(r).wait_recv()
        lax.fori_loop(2, 4, stack_row, 0)

    def turned(r, h):
        block = s9[r, h * 128:(h + 1) * 128, 512:640].astype(F32).T.astype(BF16)
        return block.reshape(RUN, SHARE, 128)

    for r in range(2):
        for h in range(2):
            at = r * 256 + h * 128
            mt[:, :, at:at + 128] = turned(2 + r, h)

    @when(odd, sec > 1)
    def _():
        slab_sends(0, "wait_send")
        slab_sends(1, "wait_send")
        pl.semaphore_signal(go, inc=1, device_id=(sec - 1, j), device_id_type=MESH)

    @when(even, sec > 0)
    def _():
        pl.semaphore_wait(go, 1)

    @when(top)
    def _():
        to_skip_b().start()

    @when(sec >= 4, odd)
    def _():
        to_skip(4).start()

    @when(sec >= 4, even)
    def _():
        to_skip(2).start()

    def mx_out(d):
        return remote(mt.at[mate(d)], mrun.at[y], mx_send.at[d], mx_recv.at[d], sec, g * RUN + mate(d))

    def mx_in(d):
        return remote(mt.at[y], mrun.at[mate_in(d)], mx_send.at[d], mx_recv.at[d], sec, g * RUN + mate_in(d))

    def end_out(i, d):
        return remote(mtx.at[mate(d)], ends.at[i], end_send.at[d], end_recv.at[i], sec, g * RUN + mate(d))

    for d in FAR:
        mx_out(d).start()
    mrun[y] = mt[y]

    @when(sec == 0)
    def _():
        for r in (1, 4):
            to_sibling(r).wait_recv()
            lax.fori_loop(r, r + 1, stack_row, 0)

    for outer, r in ((both(first, low_row), 1), (both(last, high_row), 4)):
        @when(outer)
        def _():
            for h in range(2):
                mtx[:, :, h * 128:(h + 1) * 128] = turned(r, h)

    has_end = (both(first, low_row), both(last, high_row))
    for i in range(2):
        @when(has_end[i])
        def _():
            for d in range(1, RUN):
                end_out(i, d).start()
            ends[i] = mtx[y]

    @when(sec >= n_sec - 2)
    def _():
        gather_run((0, 1))

    @when(sec >= n_sec // 2)
    def _():
        gather_run((2, 3))

    lane = lax.broadcasted_iota(jnp.int32, (SHARE, 512), 1)
    cell_x = lax.rem(lax.div(lane, 8), 32)
    cell_z = lax.rem(lane, 8)
    fits = []
    for dx in (-1, 0, 1):
        for dz in (-1, 0, 1):
            fits.append(both(cell_x - dx >= 0, cell_x - dx < 32, cell_z - dz >= 0, cell_z - dz < 8))

    def spread(m, slot, width):
        for i, ok in enumerate(fits):
            step = ((i // 3 - 1) * 8 + i % 3 - 1) % width
            moved = m if step == 0 else jnp.where(ok[:, :width], pltpu.roll(m, step, 1), 0.0)
            lhs[slot, i * SHARE:(i + 1) * SHARE, 0:width] = moved.astype(BF16)

    bias = jnp.zeros((SHARE, 512), F32)
    terms = [jnp.zeros((9 * SHARE, 128), F32)] * 3
    for n, d in enumerate((0, 1, 7, 2, 6, 3, 5, 4)):
        if d > 0:
            mx_in(d).wait_recv()
        u = mate_in(d)
        m = mrun[u].astype(F32)
        bias = bias + m
        spread(m, n, 512)
        for dy in range(3):
            terms[dy] = terms[dy] + jnp.dot(
                lhs[n], srun[pl.ds(2 * u + dy, 2)].reshape(512, 128), preferred_element_type=F32
            )
    for i, (there, away) in enumerate(((low_row, y > 0), (high_row, y < RUN - 1))):
        @when(there, away)
        def _():
            end_out(i, 1).wait_recv()

        spread(ends[i].astype(F32), RUN + i, 256)
        dy, row = ((2, 1), (0, 2 * RUN))[i]
        terms[dy] = terms[dy] + jnp.dot(
            lhs[RUN + i, :, 0:256], srun[row], preferred_element_type=F32
        )

    column = lax.broadcasted_iota(jnp.int32, (SHARE, 128), 1)

    def split(total):
        head = total.astype(BF16).astype(F32)
        return jnp.where(column == 0, head, jnp.where(column == 1, total - head, 0.0))

    for dy in range(3):
        block = terms[dy].astype(BF16)
        for i in range(9):
            t = dy * 9 + i
            kgc[t // TILES, t % TILES] = block[i * SHARE:(i + 1) * SHARE]
    kgc[WIDE - 1, TILES - 1] = split(jnp.sum(bias, axis=1, keepdims=True)).astype(BF16)

    def rs_out(d):
        return remote(
            kgc.at[lax.div(peer(d), 2)], rsb.at[g], rs_send.at[d], rs_recv.at[d], sec, peer(d) * RUN + y
        )

    def rs_in(d):
        return remote(
            kgc.at[0], rsb.at[peer_in(d)], rs_send.at[d], rs_recv.at[d], sec, peer_in(d) * RUN + y
        )

    for d in FAR_RUNS:
        rs_out(d).start()
    rsb[g] = kgc[x]

    @when(sec == 0)
    def _():
        to_skip(2).wait_recv()
        layer(mine, 2, 4, [(lambda: None, (1, 2, 3, 4))], lambda r: None)

    def beside(d):
        return lax.rem(x + d, WIDE)

    def beside_in(d):
        return lax.rem(x + WIDE - d, WIDE)

    def across(at):
        return (2 * at + high) * RUN + y

    def a1_out(d):
        part = a1.at[y, x]
        return remote(part, part, a1_send.at[d], a1_recv.at[d], sec, across(beside(d)))

    def a1_in(d):
        part = a1.at[y, beside_in(d)]
        return remote(part, part, a1_send.at[d], a1_recv.at[d], sec, across(beside_in(d)))

    def b1_out(d):
        return remote(a1.at[y], a1.at[y], b1_send.at[d], b1_recv.at[d], sec, g * RUN + mate(d))

    def b1_in(d):
        part = a1.at[mate_in(d)]
        return remote(part, part, b1_send.at[d], b1_recv.at[d], sec, g * RUN + mate_in(d))

    def a2_out(d):
        part = a2.at[x, y]
        return remote(part, part, a2_send.at[d], a2_recv.at[d], sec, g * RUN + mate(d))

    def a2_in(d):
        part = a2.at[x, mate_in(d)]
        return remote(part, part, a2_send.at[d], a2_recv.at[d], sec, g * RUN + mate_in(d))

    def b2_out(d):
        return remote(a2.at[x], a2.at[x], b2_send.at[d], b2_recv.at[d], sec, across(beside(d)))

    def b2_in(d):
        part = a2.at[beside_in(d)]
        return remote(part, part, b2_send.at[d], b2_recv.at[d], sec, across(beside_in(d)))

    for d in range(1, GROUPS):
        rs_in(d).wait_recv()
    total = rsb[0].astype(F32)
    for d in range(1, GROUPS):
        total = total + rsb[d].astype(F32)
    final = total[TILES - 1]
    pair = split(final[:, 0:1] + final[:, 1:2])
    a1[y, x] = total[:AHEAD].astype(BF16)
    a2[x, y, 0:TILES - 1 - AHEAD] = total[AHEAD:TILES - 1].astype(BF16)
    a2[x, y, TILES - 1 - AHEAD] = jnp.where(x == WIDE - 1, pair, final).astype(BF16)
    for d in range(1, WIDE):
        a1_out(d).start()
    for d in FAR:
        a2_out(d).start()
    act_ref[...] = act6[2:4].reshape(act_ref.shape)
    for d in range(1, WIDE):
        a1_in(d).wait_recv()
    for d in FAR:
        b1_out(d).start()
    for d in range(1, RUN):
        a2_in(d).wait_recv()
    for d in range(1, WIDE):
        b2_out(d).start()

    halo_do(True, has_low, "wait_send")
    halo_do(False, has_high, "wait_send")

    for step in range(4):
        up_out(step).wait_send()
        if step < 3:
            down_out(step).wait_send()

    @when(odd)
    def _():
        for r in range(1, 5):
            to_sibling(r).wait_send()

    @when(even, sec > 0)
    def _():
        to_pair(0).wait_send()
        to_pair(1).wait_send()

    @when(top)
    def _():
        to_skip_b().wait_send()

    @when(sec >= 4, odd)
    def _():
        to_skip(4).wait_send()

    @when(sec >= 4, even)
    def _():
        to_skip(2).wait_send()

    for i in range(2):
        @when(has_end[i])
        def _():
            for d in range(1, RUN):
                end_out(i, d).wait_send()

    for d in range(1, RUN):
        mx_out(d).wait_send()
        rs_out(d).wait_send()
        a2_out(d).wait_send()
        b1_out(d).wait_send()
    for d in range(1, WIDE):
        a1_out(d).wait_send()
        b2_out(d).wait_send()
        b2_in(d).wait_recv()
    for d in range(1, RUN):
        b1_in(d).wait_recv()


def finish(norm_factor, act_in, a1, a2, act_ref, kg_ref, bias_ref):
    act_ref[...] = act_in[...]
    for t in range(WIDE * TILES):
        q, i = t // TILES, t % TILES
        tile = a1[:, q, i] if i < AHEAD else a2[q, :, i - AHEAD]
        tile = tile.reshape(128, 128).astype(F32).T * norm_factor
        if t < 27:
            kg_ref[0, t] = tile
        else:
            bias_ref[...] = tile[0:1] + tile[1:2]


def local(saved_in, saved_out, weights, cotangent):
    rows_y, cells_x, cells_z, channels = cotangent.shape
    norm_factor = 1.0 / math.sqrt(rows_y * lax.axis_size("slab") * cells_x * cells_z)
    flat = (rows_y, cells_x * cells_z, channels)
    vmem = pl.BlockSpec(memory_space=pltpu.VMEM)
    hbm = pl.BlockSpec(memory_space=pl.ANY)
    six = pltpu.VMEM((6, 256, 128), BF16)
    two = pltpu.VMEM((2, 256, 128), BF16)
    sems = pltpu.SemaphoreType.DMA
    act, a1, a2 = pl.pallas_call(
        kernel,
        name="backward",
        out_shape=(
            jax.ShapeDtypeStruct((1,) + cotangent.shape, BF16),
            jax.ShapeDtypeStruct((RUN, WIDE, AHEAD, SHARE, channels), BF16),
            jax.ShapeDtypeStruct((WIDE, RUN, TILES - AHEAD, SHARE, channels), BF16),
        ),
        in_specs=[hbm] * 4,
        out_specs=(vmem,) * 3,
        scratch_shapes=[
            pltpu.VMEM((27, 128, 128), BF16), two, two,
            six, six, six, six,
            pltpu.VMEM((6, 256, 1152), BF16),
            pltpu.VMEM((1152, 384), BF16),
            six, six, six,
            pltpu.VMEM((6, 256, 1152), BF16),
            pltpu.VMEM((1152, 384), BF16),
            pltpu.VMEM((RUN, SHARE, 512), BF16),
            pltpu.VMEM((RUN, SHARE, 256), BF16),
            pltpu.VMEM((RUN, SHARE, 512), BF16),
            pltpu.VMEM((2, SHARE, 256), BF16),
            pltpu.VMEM((RUN + 2, 9 * SHARE, 512), BF16),
            pltpu.VMEM((2 * RUN + 2, 256, 128), BF16),
            pltpu.VMEM((WIDE, TILES, SHARE, 128), BF16),
            pltpu.VMEM((GROUPS, TILES, SHARE, 128), BF16),
            sems((4,)), sems((2,)), sems((2,)),
            sems((4,)), sems((4,)), sems((6,)), sems((6,)), sems, sems((2,)),
            sems((2,)), sems((2,)), sems, sems,
            pltpu.SemaphoreType.REGULAR,
            sems((4,)), sems((4,)), sems((3,)), sems((3,)), sems((8,)), sems((2,)),
            sems((8,)), sems((8,)), sems((8,)), sems((8,)),
            sems((8,)), sems((8,)), sems((8,)), sems((8,)),
            sems((8,)), sems((8,)), sems((8,)), sems((8,)),
        ],
        compiler_params=pltpu.CompilerParams(
            collective_id=0, has_side_effects=True, vmem_limit_bytes=56 << 20
        ),
    )(
        saved_in[0].reshape(flat), saved_out[0].reshape(flat), weights[0], cotangent.reshape(flat)
    )
    return pl.pallas_call(
        functools.partial(finish, norm_factor),
        name="finish",
        out_shape=(
            jax.ShapeDtypeStruct((1,) + cotangent.shape, BF16),
            jax.ShapeDtypeStruct((1, 27, channels, channels), F32),
            jax.ShapeDtypeStruct((1, channels), F32),
        ),
        in_specs=[vmem] * 3,
        out_specs=(vmem,) * 3,
    )(act, a1, a2)


def solution(mesh):
    placed = (
        P("section", "slab", None, None, None),
        P("section", "slab", None, None, None),
        P("section", None, None, None),
        P("slab", None, None, None),
    )
    return jax.shard_map(
        local,
        mesh=mesh,
        in_specs=placed,
        out_specs=(
            P("section", "slab", None, None, None),
            P("section", None, None, None),
            P("section", None),
        ),
        check_vma=False,
    )
```

```python
import functools
import math

import jax
import jax.numpy as jnp
from jax import lax
from jax.experimental import pallas as pl
from jax.experimental.pallas import tpu as pltpu
from jax.sharding import PartitionSpec as P

MESH = pl.DeviceIdType.MESH
F32 = jnp.float32
BF16 = jnp.bfloat16

RUN = 8
GROUPS = 8
SHARE = 16
WIDE = 4
TILES = 7
FAR = (4, 3, 5, 2, 6, 1, 7)
FAR_RUNS = (3, 5, 1, 7, 4, 2, 6)
AHEAD = 3


def kernel(
    si_ref, so_ref, w_ref, cot_ref,
    act_ref, a1, a2,
    wv, sov, cotv, inc, so6, act6, skip6, s9, w9, sob, act6b, skip6b, s9b, w9b, mt, mtx, mrun, ends, lhs, srun, kgc, rsb,
    load, halo_send, halo_recv, row_send, row_recv, slab_send, slab_recv, skip_send, skip_recv,
    pair_send, pair_recv, skip_send_b, skip_recv_b, go,
    up_send, up_recv, down_send, down_recv, end_send, end_recv,
    mx_send, mx_recv, rs_send, rs_recv,
    a1_send, a1_recv, b1_send, b1_recv, a2_send, a2_recv, b2_send, b2_recv,
):
    sec = lax.axis_index("section")
    j = lax.axis_index("slab")
    n_sec = lax.axis_size("section")
    n_slab = lax.axis_size("slab")
    y = lax.rem(j, RUN)
    g = lax.div(j, RUN)
    odd = lax.rem(sec, 2) == 1
    even = lax.rem(sec, 2) == 0
    has_low = j > 0
    has_high = j < n_slab - 1
    top = sec == n_sec - 1
    first = y == 0
    last = y == RUN - 1
    x = lax.div(g, 2)
    high = lax.rem(g, 2)

    def both(*conditions):
        out = jnp.bool_(conditions[0]) if conditions[0] is True else conditions[0]
        for c in conditions[1:]:
            out = jnp.logical_and(out, c)
        return out

    def when(*conditions):
        return pl.when(both(*conditions))

    def loads():
        return (
            pltpu.make_async_copy(so_ref, sov, load.at[0]),
            pltpu.make_async_copy(cot_ref, cotv, load.at[1]),
            pltpu.make_async_copy(w_ref, wv, load.at[2]),
            pltpu.make_async_copy(si_ref, srun.at[pl.ds(1 + 2 * y, 2)], load.at[3]),
        )

    for c in loads():
        c.start()

    barrier = pltpu.get_barrier_semaphore()

    def signal(s, t):
        pl.semaphore_signal(barrier, inc=1, device_id=(s, t), device_id_type=MESH)

    @when(has_low, first)
    def _():
        signal(sec, j - 1)

    @when(has_high, last)
    def _():
        signal(sec, j + 1)

    for d in range(1, RUN):
        signal(sec, g * RUN + lax.rem(y + d, RUN))
    for d in range(1, GROUPS):
        signal(sec, lax.rem(g + d, GROUPS) * RUN + y)

    @when(sec > 0)
    def _():
        signal(sec - 1, j)

    @when(jnp.logical_not(top))
    def _():
        signal(sec + 1, j)

    for step, there in ((-2, both(odd, sec > 1)), (2, both(odd, jnp.logical_not(top)))):
        @when(there)
        def _():
            signal(sec + step, j)

        @when(there, has_low)
        def _():
            signal(sec + step, j - 1)

        @when(there, has_high)
        def _():
            signal(sec + step, j + 1)

    @when(sec >= 4)
    def _():
        signal(sec - 4, j)

    @when(sec < 4)
    def _():
        signal(sec + 4, j)

    def one(*conditions):
        return jnp.where(both(*conditions), 1, 0)

    pairs = one(odd, sec > 1) + one(odd, jnp.logical_not(top))
    expected = (
        RUN - 1 + GROUPS - 1 + 1
        + one(has_low, first) + one(has_high, last)
        + one(sec > 0) + one(jnp.logical_not(top))
        + pairs * (1 + one(has_low) + one(has_high))
    )

    blank = jnp.zeros((2, 256, 128), BF16)

    @when(jnp.logical_not(has_low))
    def _():
        so6[0:2] = blank

        @when(odd)
        def _():
            inc[0:2] = blank

    @when(jnp.logical_not(has_high))
    def _():
        so6[4:6] = blank

        @when(odd)
        def _():
            inc[4:6] = blank

    srun[0] = blank[0]
    srun[2 * RUN + 1] = blank[0]

    @when(g == 0)
    def _():
        ends[0] = jnp.zeros((SHARE, 256), BF16)

    @when(g == GROUPS - 1)
    def _():
        ends[1] = jnp.zeros((SHARE, 256), BF16)

    load_so, load_cot, load_w, load_si = loads()
    load_so.wait()
    load_cot.wait()

    @when(top)
    def _():
        so6[2:4] = jnp.where(sov[...].astype(F32) > 0, cotv[...].astype(F32), 0.0).astype(BF16)

    @when(jnp.logical_not(top))
    def _():
        so6[2:4] = sov[...]

    load_si.wait()

    pl.semaphore_wait(barrier, expected)

    def remote(src, dst, ss, rs, s, t):
        return pltpu.make_async_remote_copy(
            src_ref=src, dst_ref=dst, send_sem=ss, recv_sem=rs,
            device_id=(s, t), device_id_type=MESH,
        )

    def halo(low, rows):
        if low:
            here, there = ((pl.ds(2, 2), pl.ds(4, 2)), (2, 4))[2 - rows]
        else:
            here, there = ((pl.ds(2, 2), pl.ds(0, 2)), (3, 1))[2 - rows]
        i = 0 if low else 1
        return remote(
            so6.at[here], so6.at[there], halo_send.at[i], halo_recv.at[i], sec, j - 1 if low else j + 1
        )

    def halo_do(low, there, act):
        for rows, parity in ((2, odd), (1, even)):
            @when(there, parity)
            def _():
                getattr(halo(low, rows), act)()

    halo_do(True, has_low, "start")
    halo_do(False, has_high, "start")

    load_w.wait()

    def turn(k, carry):
        dy, dx, dz = lax.div(k, 9), lax.rem(lax.div(k, 3), 3), lax.rem(k, 3)
        tile = wv[k].astype(F32).T.astype(BF16)
        rows = pl.ds(pl.multiple_of(dx * 384 + dz * 128, 128), 128)
        w9[rows, pl.ds(pl.multiple_of(dy * 128, 128), 128)] = tile
        return carry

    lax.fori_loop(0, 27, turn, 0)
    def to_pair(i):
        if i == 0:
            return remote(w9, w9b, pair_send.at[0], pair_recv.at[0], sec + 1, j)
        return remote(so6.at[1:5], sob.at[1:5], pair_send.at[1], pair_recv.at[1], sec + 1, j)

    @when(even, sec > 0)
    def _():
        to_pair(0).start()

    def mate(d):
        return lax.rem(y + d, RUN)

    def mate_in(d):
        return lax.rem(y + RUN - d, RUN)

    def peer(d):
        return lax.rem(g + d, GROUPS)

    def peer_in(d):
        return lax.rem(g + GROUPS - d, GROUPS)

    def rows_of(origin):
        return srun.at[pl.ds(1 + 2 * origin, 2)]

    def up_out(step):
        rows = rows_of(lax.rem(y + RUN - step, RUN))
        return remote(rows, rows, up_send.at[step], up_recv.at[step], sec, g * RUN + mate(1))

    def up_in(step):
        rows = rows_of(lax.rem(y + RUN - step - 1, RUN))
        return remote(rows, rows, up_send.at[step], up_recv.at[step], sec, g * RUN + mate(1))

    def down_out(step):
        rows = rows_of(lax.rem(y + step, RUN))
        return remote(rows, rows, down_send.at[step], down_recv.at[step], sec, g * RUN + mate(RUN - 1))

    def down_in(step):
        rows = rows_of(lax.rem(y + step + 1, RUN))
        return remote(rows, rows, down_send.at[step], down_recv.at[step], sec, g * RUN + mate(RUN - 1))

    low_row = g > 0
    high_row = g < GROUPS - 1

    def gather_run(steps):
        for step in steps:
            up_out(step).start()
            if step < 3:
                down_out(step).start()
            up_in(step).wait_recv()
            if step < 3:
                down_in(step).wait_recv()

    def halo_wait(low):
        halo_do(not low, has_low if low else has_high, "wait_recv")

    @when(even)
    def _():
        halo_wait(True)
        halo_wait(False)

    @when(even, sec > 0)
    def _():
        to_pair(1).start()

    @when(sec < n_sec - 2)
    def _():
        gather_run((0, 1))

    @when(sec < n_sec // 2)
    def _():
        gather_run((2, 3))

    def to_sibling(r):
        return remote(act6.at[r], inc.at[r], row_send.at[r - 1], row_recv.at[r - 1], sec - 1, j)

    def to_slab(i, which):
        at = (2, 4, 0)[which] + i
        k = 3 * i + which
        return remote(
            act6b.at[2 + i], inc.at[at], slab_send.at[k], slab_recv.at[k], sec - 2, j + (0, -1, 1)[which]
        )

    def slab_sends(i, act, order=(1, 2, 0)):
        for which in order:
            @when((True, has_low, has_high)[which])
            def _():
                getattr(to_slab(i, which), act)()

    def to_skip(rows):
        if rows == 4:
            return remote(act6.at[1:5], skip6.at[1:5], skip_send, skip_recv.at[0], sec - 4, j)
        return remote(act6.at[2:4], skip6.at[2:4], skip_send, skip_recv.at[1], sec - 4, j)

    def to_skip_b():
        return remote(act6b.at[2:4], skip6b.at[2:4], skip_send_b, skip_recv_b, sec - 4, j)

    depth = lax.broadcasted_iota(jnp.int32, (32, 8, 128), 1)
    edge_x = jnp.zeros((8, 128), F32)

    def stack_row(r, carry):
        held = so6[r].astype(F32)
        arrived = jnp.where(held > 0, inc[r].astype(F32), 0.0)
        put_row(s9, r, jnp.where(top, held, arrived))
        return carry

    def stack_pair(r, carry):
        put_row(s9b, r, jnp.where(sob[r].astype(F32) > 0, act6[r].astype(F32), 0.0))
        return carry

    def put_row(s9, r, m):
        m = m.reshape(32, 8, 128)
        up = jnp.where(depth == 7, 0.0, pltpu.roll(m, 7, 1)).reshape(256, 128)
        down = jnp.where(depth == 0, 0.0, pltpu.roll(m, 1, 1)).reshape(256, 128)
        for b, v in enumerate((up, m.reshape(256, 128), down)):
            at = b * 128
            s9[r, :, at:at + 128] = jnp.concatenate([v[8:], edge_x], 0).astype(BF16)
            s9[r, :, at + 384:at + 512] = v.astype(BF16)
            s9[r, :, at + 768:at + 896] = jnp.concatenate([edge_x, v[:-8]], 0).astype(BF16)

    mine = (s9, w9, skip6, act6)
    pair = (s9b, w9b, skip6b, act6b)

    def layer(refs, lo, hi, steps, done):
        s9, w9, skip6, act6 = refs
        sums, count = {}, {}
        for ready, rows in steps:
            ready()
            for t in rows:
                reach = [dy for dy in (-1, 0, 1) if lo <= t + dy < hi]
                p = jnp.dot(
                    s9[t], w9[:, (reach[0] + 1) * 128:(reach[-1] + 2) * 128],
                    preferred_element_type=F32,
                )
                for i, dy in enumerate(reach):
                    r = t + dy
                    v = p[:, i * 128:(i + 1) * 128]
                    sums[r] = sums[r] + v if r in sums else v
                    count[r] = count.get(r, 0) + 1
                    if count[r] == 3:
                        total = sums.pop(r)
                        total = jnp.where(sec < 4, total + skip6[r].astype(F32), total)
                        act6[r] = total.astype(BF16)
                        done(r)

    def odd_layer(low_first):
        def own():
            @when(jnp.logical_not(top))
            def _():
                to_slab(0, 0).wait_recv()
                to_slab(1, 0).wait_recv()

            lax.fori_loop(2, 4, stack_row, 0)

        def side(low):
            halo_wait(low)

            @when(jnp.logical_not(top), has_low if low else has_high)
            def _():
                for i in range(2):
                    to_slab(i, 2 if low else 1).wait_recv()

            at = 0 if low else 4
            lax.fori_loop(at, at + 2, stack_row, 0)

        @when(sec < 4)
        def _():
            to_skip(4).wait_recv()

        lows = (lambda: side(True), (0, 1))
        highs = (lambda: side(False), (4, 5))
        order = [lows, highs] if low_first else [highs, lows]
        layer(mine, 1, 5, [(own, (2, 3))] + order, lambda r: to_sibling(r).start())

        @when(sec > 1)
        def _():
            to_pair(0).wait_recv()
            to_pair(1).wait_recv()

            @when(sec < 4)
            def _():
                to_skip_b().wait_recv()

            rows = (1, 2, 3, 4) if low_first else (4, 3, 2, 1)
            layer(
                pair, 2, 4,
                [(lambda r=r: lax.fori_loop(r, r + 1, stack_pair, 0), (r,)) for r in rows],
                lambda r: slab_sends(r - 2, "start", (2, 1, 0) if low_first else (1, 2, 0)),
            )

    def even_layer(low_first):
        rows = (1, 2, 3, 4) if low_first else (4, 3, 2, 1)

        def ready(r):
            to_sibling(r).wait_recv()
            lax.fori_loop(r, r + 1, stack_row, 0)

        @when(sec < 4)
        def _():
            to_skip(2).wait_recv()

        layer(mine, 2, 4, [(lambda r=r: ready(r), (r,)) for r in rows], lambda r: None)

    @when(odd, first)
    def _():
        odd_layer(False)

    @when(odd, jnp.logical_not(first))
    def _():
        odd_layer(True)

    @when(even, sec > 0, first)
    def _():
        even_layer(False)

    @when(even, sec > 0, jnp.logical_not(first))
    def _():
        even_layer(True)

    @when(sec == 0)
    def _():
        for r in (2, 3):
            to_sibling(r).wait_recv()
        lax.fori_loop(2, 4, stack_row, 0)

    def turned(r, h):
        block = s9[r, h * 128:(h + 1) * 128, 512:640].astype(F32).T.astype(BF16)
        return block.reshape(RUN, SHARE, 128)

    for r in range(2):
        for h in range(2):
            at = r * 256 + h * 128
            mt[:, :, at:at + 128] = turned(2 + r, h)

    @when(odd, sec > 1)
    def _():
        slab_sends(0, "wait_send")
        slab_sends(1, "wait_send")
        pl.semaphore_signal(go, inc=1, device_id=(sec - 1, j), device_id_type=MESH)

    @when(even, sec > 0)
    def _():
        pl.semaphore_wait(go, 1)

    @when(top)
    def _():
        to_skip_b().start()

    @when(sec >= 4, odd)
    def _():
        to_skip(4).start()

    @when(sec >= 4, even)
    def _():
        to_skip(2).start()

    def mx_out(d):
        return remote(mt.at[mate(d)], mrun.at[y], mx_send.at[d], mx_recv.at[d], sec, g * RUN + mate(d))

    def mx_in(d):
        return remote(mt.at[y], mrun.at[mate_in(d)], mx_send.at[d], mx_recv.at[d], sec, g * RUN + mate_in(d))

    def end_out(i, d):
        return remote(mtx.at[mate(d)], ends.at[i], end_send.at[d], end_recv.at[i], sec, g * RUN + mate(d))

    for d in FAR:
        mx_out(d).start()
    mrun[y] = mt[y]

    @when(sec == 0)
    def _():
        for r in (1, 4):
            to_sibling(r).wait_recv()
            lax.fori_loop(r, r + 1, stack_row, 0)

    for outer, r in ((both(first, low_row), 1), (both(last, high_row), 4)):
        @when(outer)
        def _():
            for h in range(2):
                mtx[:, :, h * 128:(h + 1) * 128] = turned(r, h)

    has_end = (both(first, low_row), both(last, high_row))
    for i in range(2):
        @when(has_end[i])
        def _():
            for d in range(1, RUN):
                end_out(i, d).start()
            ends[i] = mtx[y]

    @when(sec >= n_sec - 2)
    def _():
        gather_run((0, 1))

    @when(sec >= n_sec // 2)
    def _():
        gather_run((2, 3))

    lane = lax.broadcasted_iota(jnp.int32, (SHARE, 512), 1)
    cell_x = lax.rem(lax.div(lane, 8), 32)
    cell_z = lax.rem(lane, 8)
    fits = []
    for dx in (-1, 0, 1):
        for dz in (-1, 0, 1):
            fits.append(both(cell_x - dx >= 0, cell_x - dx < 32, cell_z - dz >= 0, cell_z - dz < 8))

    def spread(m, slot, width):
        for i, ok in enumerate(fits):
            step = ((i // 3 - 1) * 8 + i % 3 - 1) % width
            moved = m if step == 0 else jnp.where(ok[:, :width], pltpu.roll(m, step, 1), 0.0)
            lhs[slot, i * SHARE:(i + 1) * SHARE, 0:width] = moved.astype(BF16)

    bias = jnp.zeros((SHARE, 512), F32)
    terms = [jnp.zeros((9 * SHARE, 128), F32)] * 3
    for n, d in enumerate((0, 1, 7, 2, 6, 3, 5, 4)):
        if d > 0:
            mx_in(d).wait_recv()
        u = mate_in(d)
        m = mrun[u].astype(F32)
        bias = bias + m
        spread(m, n, 512)
        for dy in range(3):
            terms[dy] = terms[dy] + jnp.dot(
                lhs[n], srun[pl.ds(2 * u + dy, 2)].reshape(512, 128), preferred_element_type=F32
            )
    for i, (there, away) in enumerate(((low_row, y > 0), (high_row, y < RUN - 1))):
        @when(there, away)
        def _():
            end_out(i, 1).wait_recv()

        spread(ends[i].astype(F32), RUN + i, 256)
        dy, row = ((2, 1), (0, 2 * RUN))[i]
        terms[dy] = terms[dy] + jnp.dot(
            lhs[RUN + i, :, 0:256], srun[row], preferred_element_type=F32
        )

    column = lax.broadcasted_iota(jnp.int32, (SHARE, 128), 1)

    def split(total):
        head = total.astype(BF16).astype(F32)
        return jnp.where(column == 0, head, jnp.where(column == 1, total - head, 0.0))

    for dy in range(3):
        block = terms[dy].astype(BF16)
        for i in range(9):
            t = dy * 9 + i
            kgc[t // TILES, t % TILES] = block[i * SHARE:(i + 1) * SHARE]
    kgc[WIDE - 1, TILES - 1] = split(jnp.sum(bias, axis=1, keepdims=True)).astype(BF16)

    def rs_out(d):
        return remote(
            kgc.at[lax.div(peer(d), 2)], rsb.at[g], rs_send.at[d], rs_recv.at[d], sec, peer(d) * RUN + y
        )

    def rs_in(d):
        return remote(
            kgc.at[0], rsb.at[peer_in(d)], rs_send.at[d], rs_recv.at[d], sec, peer_in(d) * RUN + y
        )

    for d in FAR_RUNS:
        rs_out(d).start()
    rsb[g] = kgc[x]

    @when(sec == 0)
    def _():
        to_skip(2).wait_recv()
        layer(mine, 2, 4, [(lambda: None, (1, 2, 3, 4))], lambda r: None)

    def beside(d):
        return lax.rem(x + d, WIDE)

    def beside_in(d):
        return lax.rem(x + WIDE - d, WIDE)

    def across(at):
        return (2 * at + high) * RUN + y

    def a1_out(d):
        part = a1.at[y, x]
        return remote(part, part, a1_send.at[d], a1_recv.at[d], sec, across(beside(d)))

    def a1_in(d):
        part = a1.at[y, beside_in(d)]
        return remote(part, part, a1_send.at[d], a1_recv.at[d], sec, across(beside_in(d)))

    def b1_out(d):
        return remote(a1.at[y], a1.at[y], b1_send.at[d], b1_recv.at[d], sec, g * RUN + mate(d))

    def b1_in(d):
        part = a1.at[mate_in(d)]
        return remote(part, part, b1_send.at[d], b1_recv.at[d], sec, g * RUN + mate_in(d))

    def a2_out(d):
        part = a2.at[x, y]
        return remote(part, part, a2_send.at[d], a2_recv.at[d], sec, g * RUN + mate(d))

    def a2_in(d):
        part = a2.at[x, mate_in(d)]
        return remote(part, part, a2_send.at[d], a2_recv.at[d], sec, g * RUN + mate_in(d))

    def b2_out(d):
        return remote(a2.at[x], a2.at[x], b2_send.at[d], b2_recv.at[d], sec, across(beside(d)))

    def b2_in(d):
        part = a2.at[beside_in(d)]
        return remote(part, part, b2_send.at[d], b2_recv.at[d], sec, across(beside_in(d)))

    for d in range(1, GROUPS):
        rs_in(d).wait_recv()
    total = rsb[0].astype(F32)
    for d in range(1, GROUPS):
        total = total + rsb[d].astype(F32)
    final = total[TILES - 1]
    pair = split(final[:, 0:1] + final[:, 1:2])
    a1[y, x] = total[:AHEAD].astype(BF16)
    a2[x, y, 0:TILES - 1 - AHEAD] = total[AHEAD:TILES - 1].astype(BF16)
    a2[x, y, TILES - 1 - AHEAD] = jnp.where(x == WIDE - 1, pair, final).astype(BF16)
    for d in range(1, WIDE):
        a1_out(d).start()
    for d in FAR:
        a2_out(d).start()
    act_ref[...] = act6[2:4].reshape(act_ref.shape)
    for d in range(1, WIDE):
        a1_in(d).wait_recv()
    for d in FAR:
        b1_out(d).start()
    for d in range(1, RUN):
        a2_in(d).wait_recv()
    for d in range(1, WIDE):
        b2_out(d).start()

    halo_do(True, has_low, "wait_send")
    halo_do(False, has_high, "wait_send")

    for step in range(4):
        up_out(step).wait_send()
        if step < 3:
            down_out(step).wait_send()

    @when(odd)
    def _():
        for r in range(1, 5):
            to_sibling(r).wait_send()

    @when(even, sec > 0)
    def _():
        to_pair(0).wait_send()
        to_pair(1).wait_send()

    @when(top)
    def _():
        to_skip_b().wait_send()

    @when(sec >= 4, odd)
    def _():
        to_skip(4).wait_send()

    @when(sec >= 4, even)
    def _():
        to_skip(2).wait_send()

    for i in range(2):
        @when(has_end[i])
        def _():
            for d in range(1, RUN):
                end_out(i, d).wait_send()

    for d in range(1, RUN):
        mx_out(d).wait_send()
        rs_out(d).wait_send()
        a2_out(d).wait_send()
        b1_out(d).wait_send()
    for d in range(1, WIDE):
        a1_out(d).wait_send()
        b2_out(d).wait_send()
        b2_in(d).wait_recv()
    for d in range(1, RUN):
        b1_in(d).wait_recv()


def finish(norm_factor, act_in, a1, a2, act_ref, kg_ref, bias_ref):
    act_ref[...] = act_in[...]
    for t in range(WIDE * TILES):
        q, i = t // TILES, t % TILES
        tile = a1[:, q, i] if i < AHEAD else a2[q, :, i - AHEAD]
        tile = tile.reshape(128, 128).astype(F32).T * norm_factor
        if t < 27:
            kg_ref[0, t] = tile
        else:
            bias_ref[...] = tile[0:1] + tile[1:2]


def local(saved_in, saved_out, weights, cotangent):
    rows_y, cells_x, cells_z, channels = cotangent.shape
    norm_factor = 1.0 / math.sqrt(rows_y * lax.axis_size("slab") * cells_x * cells_z)
    flat = (rows_y, cells_x * cells_z, channels)
    vmem = pl.BlockSpec(memory_space=pltpu.VMEM)
    hbm = pl.BlockSpec(memory_space=pl.ANY)
    six = pltpu.VMEM((6, 256, 128), BF16)
    two = pltpu.VMEM((2, 256, 128), BF16)
    sems = pltpu.SemaphoreType.DMA
    act, a1, a2 = pl.pallas_call(
        kernel,
        name="backward",
        out_shape=(
            jax.ShapeDtypeStruct((1,) + cotangent.shape, BF16),
            jax.ShapeDtypeStruct((RUN, WIDE, AHEAD, SHARE, channels), BF16),
            jax.ShapeDtypeStruct((WIDE, RUN, TILES - AHEAD, SHARE, channels), BF16),
        ),
        in_specs=[hbm] * 4,
        out_specs=(vmem,) * 3,
        scratch_shapes=[
            pltpu.VMEM((27, 128, 128), BF16), two, two,
            six, six, six, six,
            pltpu.VMEM((6, 256, 1152), BF16),
            pltpu.VMEM((1152, 384), BF16),
            six, six, six,
            pltpu.VMEM((6, 256, 1152), BF16),
            pltpu.VMEM((1152, 384), BF16),
            pltpu.VMEM((RUN, SHARE, 512), BF16),
            pltpu.VMEM((RUN, SHARE, 256), BF16),
            pltpu.VMEM((RUN, SHARE, 512), BF16),
            pltpu.VMEM((2, SHARE, 256), BF16),
            pltpu.VMEM((RUN + 2, 9 * SHARE, 512), BF16),
            pltpu.VMEM((2 * RUN + 2, 256, 128), BF16),
            pltpu.VMEM((WIDE, TILES, SHARE, 128), BF16),
            pltpu.VMEM((GROUPS, TILES, SHARE, 128), BF16),
            sems((4,)), sems((2,)), sems((2,)),
            sems((4,)), sems((4,)), sems((6,)), sems((6,)), sems, sems((2,)),
            sems((2,)), sems((2,)), sems, sems,
            pltpu.SemaphoreType.REGULAR,
            sems((4,)), sems((4,)), sems((3,)), sems((3,)), sems((8,)), sems((2,)),
            sems((8,)), sems((8,)), sems((8,)), sems((8,)),
            sems((8,)), sems((8,)), sems((8,)), sems((8,)),
            sems((8,)), sems((8,)), sems((8,)), sems((8,)),
        ],
        compiler_params=pltpu.CompilerParams(
            collective_id=0, has_side_effects=True, vmem_limit_bytes=56 << 20
        ),
    )(
        saved_in[0].reshape(flat), saved_out[0].reshape(flat), weights[0], cotangent.reshape(flat)
    )
    return pl.pallas_call(
        functools.partial(finish, norm_factor),
        name="finish",
        out_shape=(
            jax.ShapeDtypeStruct((1,) + cotangent.shape, BF16),
            jax.ShapeDtypeStruct((1, 27, channels, channels), F32),
            jax.ShapeDtypeStruct((1, channels), F32),
        ),
        in_specs=[vmem] * 3,
        out_specs=(vmem,) * 3,
    )(act, a1, a2)


def solution(mesh):
    placed = (
        P("section", "slab", None, None, None),
        P("section", "slab", None, None, None),
        P("section", None, None, None),
        P("slab", None, None, None),
    )
    return jax.shard_map(
        local,
        mesh=mesh,
        in_specs=placed,
        out_specs=(
            P("section", "slab", None, None, None),
            P("section", None, None, None),
            P("section", None),
        ),
        check_vma=False,
    )
```
